32 devices in a mesh: dom: 16 (over z, y, core), rep: 2 (over x).
Axes of the slice: x: 2, y: 2, z: 4, core: 2. Of those that a mesh axis runs over, the one named last changes fastest.
Arguments:
- features: bfloat16 [8192, 768], P('dom'), may hold values from -6 to 6
- tiles: bfloat16 [64, 16, 4, 128, 128], P('dom', 'rep'), may hold values from -0.0625 to 0.0625
- tile_cols: int32 [64, 16, 4], P('dom', 'rep'), may hold values from 0 to 3
- tile_mask: int32 [64, 16, 4], P('dom', 'rep'), may hold values from 0 to 1, as said below
- weight: bfloat16 [768, 768], replicated, may hold values from -0.21875 to 0.21875
- bias: float32 [768], replicated, may hold values from -3 to 3
- cotangent: bfloat16 [8192, 768], P(('dom', 'rep')), may hold values from -0.06591797 to 0.06591797
Outputs:
- output: bfloat16 [8192, 768], P(('dom', 'rep'))
- grad_weight: float32 [768, 768], replicated
- grad_bias: float32 [768], replicated
The draws below stay inside these ranges and needn't reach their ends.
Inputs may be any that keep to these rules, and one draw needn't show every extreme that they name: `tile_mask`: for each row block and source, the live slots come first and slot 0 is always live.
All inputs are finite; a program needn't handle non-finite values.
Results may differ from the reference program's by a relative error of at most 0.02.
Values may be sent and summed in bfloat16 or wider, within the bound.
A program may use at most 128 MiB of HBM per device.

```python
import jax
import jax.numpy as jnp
from jax import lax

D = 768
TB = 128
RB = 4
K = 4
NBLK = 64
NODES = 8192
N_DOM = 16
N_REP = 2


def draw_tile_mask(key, part):
    key = jax.random.fold_in(key, 7)
    counts = jax.random.randint(key, (NBLK, N_DOM, 1), 1, K + 1)
    slots = jnp.arange(K).astype(jnp.int32)
    return (slots[None, None, :] < counts).astype(jnp.int32)


def touch_ends(array, own_key, smallest, high):
    longest = array.shape.index(max(array.shape))
    spots = []
    for shift in (0, 1):
        where = [jax.random.randint(jax.random.fold_in(own_key, axis), (), 0, length) for axis, length in enumerate(array.shape)]
        where[longest] = (where[longest] + shift) % array.shape[longest]
        spots.append(tuple(where))
    return array.at[spots[0]].set(smallest).at[spots[1]].set(high)


def block_scale(rng, extent, shards, smallest, high):
    factor_of, own = 1.0, jax.random.fold_in(rng, 6)
    for axis_at, blocks in shards:
        draws = jnp.exp(jax.random.uniform(jax.random.fold_in(own, axis_at), (blocks,), jnp.float32, smallest / len(shards), high / len(shards)))
        factor_of = factor_of * jnp.repeat(draws, extent[axis_at] // blocks).reshape([-1 if axis == axis_at else 1 for axis in range(len(extent))])
    return factor_of


def normal_values(stream_key, shape, width, bound, cuts=(), dtype=jnp.bfloat16):
    factor_of = block_scale(stream_key, shape, cuts, -0.22, 0.18) if cuts else 1.0
    array = jax.random.normal(stream_key, shape, jnp.float32) * width * factor_of
    return jnp.minimum(jnp.maximum(array, -bound), bound).astype(dtype)


def setup_inputs(seed: int = 0) -> dict:
    key_of = jax.random.split(jax.random.key(seed), 8)
    features = normal_values(key_of[0], (NODES, D), 1.0, 6.0, ((0, 16),))
    tiles = normal_values(key_of[1], (NBLK, N_DOM, K, TB, TB), (N_DOM * K * TB) ** -0.5, 0.0625, ((0, 16), (1, 2)))
    tile_cols = touch_ends(jax.random.randint(key_of[2], (NBLK, N_DOM, K), 0, RB), jax.random.fold_in(key_of[2], 1), 0, RB - 1).astype(jnp.int32)
    tile_mask = draw_tile_mask(jax.random.fold_in(key_of[7], 71), 0)
    weight = normal_values(key_of[4], (D, D), D ** -0.5, 0.21875)
    bias = normal_values(key_of[5], (D,), 0.5, 3.0, (), jnp.float32)
    cotangent = normal_values(key_of[6], (NODES, D), (1.0 / (RB * TB * N_DOM) ** 0.5), 0.06591797, ((0, 32),))
    return dict(features=features, tiles=tiles, tile_cols=tile_cols, tile_mask=tile_mask, weight=weight, bias=bias, cotangent=cotangent)


def reference(features, tiles, tile_cols, tile_mask, weight, bias, cotangent):
    blocks = features.reshape(NBLK, TB, D)
    offsets = (jnp.arange(N_DOM) * RB).astype(jnp.int32)

    def aggregate_block(packed):
        tile_set, columns, live = packed
        global_cols = (offsets[:, None] + columns).astype(jnp.int32)
        picked = blocks[global_cols].astype(jnp.float32)
        masked = tile_set.astype(jnp.float32) * live[:, :, None, None].astype(jnp.float32)
        per_source = jnp.einsum("skij,skjd->sid", masked, picked)
        grouped = jnp.sum(per_source.reshape(N_REP, N_DOM // N_REP, TB, D), axis=1)
        rounded = lax.optimization_barrier(grouped.astype(jnp.bfloat16))
        return jnp.sum(rounded.astype(jnp.float32), axis=0)

    aggregate = lax.map(aggregate_block, (tiles, tile_cols, tile_mask)).reshape(NODES, D)
    mixed = aggregate.astype(jnp.bfloat16)
    pre_act = jnp.dot(mixed, weight, preferred_element_type=jnp.float32) + bias
    output = (pre_act * jax.nn.sigmoid(pre_act)).astype(jnp.bfloat16)
    sigmoid_pre = jax.nn.sigmoid(pre_act)
    grad_pre = cotangent.astype(jnp.float32) * sigmoid_pre * (1.0 + pre_act * (1.0 - sigmoid_pre))
    grad_low = grad_pre.astype(jnp.bfloat16)
    grad_weight = jnp.dot(mixed.T, grad_low, preferred_element_type=jnp.float32)
    grad_bias = jnp.sum(grad_pre, axis=0)
    return output, grad_weight, grad_bias
```

```python
import functools

import jax
import jax.numpy as jnp
from jax import lax
from jax.experimental import pallas as pl
from jax.experimental.pallas import tpu as pltpu
from jax.sharding import PartitionSpec as P

MESH = pl.DeviceIdType.MESH
CHUNKS = 8
F32 = jnp.float32
BF16 = jnp.bfloat16


def spread(value, axis, source):
    kept = jnp.where(lax.axis_index(axis) == source, value, 0).astype(value.dtype)
    return lax.psum(kept, axis)


def section_term(source, tiles, tile_cols, tile_mask, section):
    rblocks = tiles.shape[0]
    tile_side = tiles.shape[3]
    feat_width = source.shape[1]
    source_blocks = source.reshape(source.shape[0] // tile_side, tile_side, feat_width)
    columns = lax.dynamic_index_in_dim(tile_cols, section, 1, keepdims=False)
    live = lax.dynamic_index_in_dim(tile_mask, section, 1, keepdims=False)
    tile_set = lax.dynamic_index_in_dim(tiles, section, 1, keepdims=False)
    block_ids = jnp.arange(source_blocks.shape[0])
    selector = ((columns[:, :, None] == block_ids[None, None, :]) * live[:, :, None]).astype(
        jnp.bfloat16
    )
    picked = jnp.einsum(
        "bkc,cjd->bkjd", selector, source_blocks, preferred_element_type=jnp.float32
    ).astype(jnp.bfloat16)
    summed = jnp.einsum("bkij,bkjd->bid", tile_set, picked, preferred_element_type=jnp.float32)
    return summed.reshape(rblocks * tile_side, feat_width)


def on_device(features, tiles, tile_cols, tile_mask, weight, bias, cotangent):
    sections = tiles.shape[1]
    replica = lax.axis_index("rep")
    aggregate = jnp.zeros(features.shape, jnp.float32)
    for turn_index in range(sections):
        root_index = replica * sections + turn_index
        source = spread(features, "dom", root_index)
        aggregate = aggregate + section_term(source, tiles, tile_cols, tile_mask, turn_index)
    rows_sum = lax.psum_scatter(
        aggregate.astype(jnp.bfloat16), "rep", scatter_dimension=0, tiled=True
    )
    pre_act = jnp.dot(rows_sum, weight, preferred_element_type=jnp.float32) + bias
    sigmoid_pre = jax.nn.sigmoid(pre_act)
    output = (pre_act * sigmoid_pre).astype(jnp.bfloat16)
    grad_pre = cotangent.astype(jnp.float32) * sigmoid_pre * (1.0 + pre_act * (1.0 - sigmoid_pre))
    grad_low = grad_pre.astype(jnp.bfloat16)
    local_weight = jnp.einsum("nd,ne->de", rows_sum, grad_low, preferred_element_type=jnp.float32)
    local_bias = jnp.sum(grad_pre, axis=0)
    grad_weight, grad_bias = lax.psum((local_weight, local_bias), ("dom", "rep"))
    return (output, grad_weight, grad_bias)


ORDERS = (("x", "y", "z"), ("y", "z", "x"), ("z", "x", "y"))
WAYS = {"x": 2, "y": 2, "z": 4}


def part_rows(group_rows, order, stage):
    rows = group_rows
    for axis in order[: stage + 1]:
        rows //= WAYS[axis]
    return rows


def kernel(feat_hbm, tiles_hbm, cols, mask, weight_hbm, bias_ref, cot_hbm,
           out_ref, gw_ref, gb_ref,
           s000, s001, s010, s011, s100, s101, s110, s111,
           tiles_v, weight_v, cot_v, dense, acc,
           part_out, part_in, mixed, glow,
           gacc, gsend, gcore_in, gfin, gother, gfull_in,
           rb00, rb01, rb02, rb10, rb11, rb12, rb20, rb21, rb22,
           bstate, brecv,
           lsem, zrecv, yrecv, crecv, zup, zdown, ysend, csend,
           psend, precv, gcs, gcr, rs_s, rs_r, ag_s, ag_r, fs, fr, bs, br):
    slots = [[[s000, s001], [s010, s011]], [[s100, s101], [s110, s111]]]
    rbufs = [[rb00, rb01, rb02], [rb10, rb11, rb12], [rb20, rb21, rb22]]
    me = lax.axis_index("dom")
    r = lax.axis_index("rep")
    z = lax.div(me, 4)
    y = lax.rem(lax.div(me, 2), 2)
    c = lax.rem(me, 2)
    w = z + r * (3 - 2 * z)
    dz = 1 - 2 * r
    rblocks, sections, ways, side, _ = tiles_v.shape
    rows, width = acc.shape
    crows = rows // CHUNKS
    half = rows // 2

    def dev(zz, yy, cc, rr):
        return (zz * 4 + yy * 2 + cc, rr)

    def z_peer(d):
        z2 = lax.rem(lax.div(z, 2) + d // 2, 2)
        z1 = lax.rem(lax.rem(z, 2) + d % 2, 2)
        return z2 * 2 + z1

    peers = {
        "x": [dev(z, y, c, 1 - r)],
        "y": [dev(z, 1 - y, c, r)],
        "z": [dev(z_peer(d), y, c, r) for d in (1, 2, 3)],
    }
    places = {"x": [1 - r], "y": [1 - y], "z": [z_peer(d) for d in (1, 2, 3)]}
    mine = {"x": r, "y": y, "z": z}
    other_core = dev(z, y, 1 - c, r)
    up = dev(jnp.clip(z + dz, 0, 3), y, c, r)
    down = dev(jnp.clip(z - dz, 0, 3), y, c, r)

    def remote(src, dst, ss, rs, device):
        return pltpu.make_async_remote_copy(
            src_ref=src, dst_ref=dst, send_sem=ss, recv_sem=rs, device_id=device, device_id_type=MESH
        )

    for i in range(2):
        @pl.when(w == i)
        def _():
            pltpu.make_async_copy(feat_hbm, slots[i][0][0], lsem.at[0]).start()
    tiles_load = pltpu.make_async_copy(tiles_hbm, tiles_v, lsem.at[1])
    weight_load = pltpu.make_async_copy(weight_hbm, weight_v, lsem.at[2])
    cot_load = pltpu.make_async_copy(cot_hbm, cot_v, lsem.at[3])
    tiles_load.start()
    weight_load.start()
    cot_load.start()
    barrier = pltpu.get_barrier_semaphore()
    greeted = [other_core] + peers["x"] + peers["y"] + peers["z"]
    for device in greeted:
        pl.semaphore_signal(barrier, inc=1, device_id=device, device_id_type=MESH)
    pl.semaphore_wait(barrier, len(greeted))

    def chunk(ch):
        return pl.ds(pl.multiple_of(ch * crows, crows), crows)

    def z_copy(i, at, sem, rsem, device):
        slot = slots[i][0][0]
        return remote(slot.at[at], slot.at[at], sem, rsem, device)

    def y_copy(i, at, rsem):
        return remote(slots[i][0][0].at[at], slots[i][1][0].at[at], ysend.at[i], rsem, peers["y"][0])

    def c_copy(i, j, at):
        return remote(slots[i][j][0].at[at], slots[i][j][1].at[at],
                      csend.at[2 * i + j], crecv.at[2 * i + j], other_core)

    everything = pl.ds(0, rows)
    ups = {0: w <= 2, 1: jnp.logical_and(w >= 1, w <= 2)}

    def forward(i, ch):
        at = chunk(ch)

        @pl.when(ups[i])
        def _():
            z_copy(i, at, zup.at[i], zrecv.at[i, ch], up).start()

        if i == 1:
            @pl.when(w == 1)
            def _():
                z_copy(i, at, zdown.at[0], zrecv.at[i, ch], down).start()
        y_copy(i, at, yrecv.at[i, ch]).start()
        c_copy(i, 0, at).start()

    def z_step(i, ch):
        @pl.when(w != i)
        def _():
            z_copy(i, chunk(ch), zup.at[i], zrecv.at[i, ch], up).wait_recv()
            forward(i, ch)

    def y_step(i, ch):
        y_copy(i, chunk(ch), yrecv.at[i, ch]).wait_recv()
        c_copy(i, 1, chunk(ch)).start()

    for i in range(2):
        @pl.when(w == i)
        def _():
            pltpu.make_async_copy(feat_hbm, slots[i][0][0], lsem.at[0]).wait()

            @pl.loop(0, CHUNKS)
            def _(ch):
                forward(i, ch)
    tiles_load.wait()

    def assemble(index):
        i = 1 - lax.div(index, 4)
        j = lax.rem(lax.div(index, 2), 2)
        k = lax.rem(index, 2)
        zz = i + r * (1 - 2 * i)
        section = zz * 4 + (y + j - 2 * y * j) * 2 + (c + k - 2 * c * k)

        @pl.loop(0, rblocks)
        def _(b):
            base = (b * sections + section) * ways
            tile_of = [tiles_v[b, section, t].astype(F32) for t in range(ways)]
            for block in range(rows // side):
                total = None
                for t in range(ways):
                    take = jnp.logical_and(cols[base + t] == block, mask[base + t] != 0)
                    term = tile_of[t] * jnp.where(take, 1.0, 0.0)
                    total = term if total is None else total + term
                dense[index, pl.ds(pl.multiple_of(b * side, side), side),
                      block * side:(block + 1) * side] = total.astype(BF16)

    @pl.loop(0, CHUNKS)
    def _(ch):
        z_step(1, ch)

        @pl.when(ch > 0)
        def _():
            y_step(1, ch - 1)
        assemble(ch)

    def product(i, j, k, at, lanes):
        index = (1 - i) * 4 + j * 2 + k
        return jnp.dot(dense[index, at, :], slots[i][j][k][:, lanes], preferred_element_type=F32)

    z_step(0, 0)
    y_step(1, CHUNKS - 1)
    for step in range(1, CHUNKS):
        z_step(0, step)
        y_step(0, step - 1)
        if step % 2 == 1:
            j, k = step // 4, (step // 2) % 2
            if k == 1:
                c_copy(1, j, everything).wait_recv()

            @pl.loop(0, width // 256)
            def _(n):
                lanes = pl.ds(pl.multiple_of(n * 256, 256), 256)
                term = product(1, j, k, everything, lanes)
                if step == 1:
                    acc[:, lanes] = term
                else:
                    acc[:, lanes] = acc[:, lanes] + term
    y_step(0, CHUNKS - 1)
    c_copy(0, 0, everything).wait_recv()
    c_copy(0, 1, everything).wait_recv()

    def finish(start, target):
        at = pl.ds(pl.multiple_of(start, half), half)

        @pl.loop(0, width // 256)
        def _(n):
            lanes = pl.ds(pl.multiple_of(n * 256, 256), 256)
            total = acc[at, lanes]
            for j in range(2):
                for k in range(2):
                    total = total + product(0, j, k, at, lanes)
            target[:, lanes] = total.astype(BF16)

    def p_copy(t):
        at = pl.ds(t * (half // 2), half // 2)
        return remote(part_out.at[at], part_in.at[at], psend.at[t], precv.at[t], peers["x"][0])

    finish((1 - r) * half, part_out)
    for t in range(2):
        p_copy(t).start()
    finish(r * half, mixed)
    weight_load.wait()
    cot_load.wait()

    bias_rows = jnp.zeros((8, width), F32)
    for t in range(2):
        at = slice(t * (half // 2), (t + 1) * (half // 2))
        p_copy(t).wait_recv()
        low = (mixed[at, :].astype(F32) + part_in[at, :].astype(F32)).astype(BF16)
        mixed[at, :] = low
        pre = jnp.dot(low, weight_v[...], preferred_element_type=F32) + bias_ref[...]
        sig = 1.0 / (1.0 + jnp.exp(-pre))
        out_ref[at, :] = (pre * sig).astype(BF16)
        grad = cot_v[at, :].astype(F32) * sig * (1.0 + pre * (1.0 - sig))
        glow[at, :] = grad.astype(BF16)
        bias_rows = bias_rows + jnp.sum(grad.reshape(half // 16, 8, width), axis=0)

    cw = width // 2

    def grad_half(start):
        lanes = pl.ds(pl.multiple_of(start, 128), cw)
        return lax.dot_general(mixed[...], glow[:, lanes], (((0,), (0,)), ((), ())),
                               preferred_element_type=F32)

    def b_send(stage, axis_peers, first):
        copies = []
        for d, device in enumerate(axis_peers):
            copies.append(remote(bstate.at[stage], brecv.at[first + d], bs.at[first + d],
                                 br.at[first + d], device))
            copies[-1].start()
        return copies

    def b_sum(stage, copies, first):
        for copy in copies:
            copy.wait_recv()
        total = bstate[stage] + brecv[first]
        if len(copies) == 3:
            total = total + (brecv[first + 1] + brecv[first + 2])
        bstate[stage + 1] = total

    sent = []
    bstate[0] = bias_rows
    gsend_core = gother
    gsend_core[...] = grad_half((1 - c) * cw).astype(BF16)
    core_copy = remote(gsend_core, gcore_in, gcs, gcr, other_core)
    core_copy.start()
    b_copies = b_send(0, [other_core], 0)
    gacc[...] = grad_half(c * cw)
    core_copy.wait_recv()
    gacc[...] = gacc[...] + gcore_in[...].astype(F32)
    b_sum(0, b_copies, 0)
    sent += [core_copy] + b_copies

    group_rows = width // 3
    starts = [g * group_rows for g in range(3)]
    history = [[], [], []]
    b_first = (1, 2, 3)
    for stage in range(3):
        flying = []
        for g, order in enumerate(ORDERS):
            axis = order[stage]
            size = part_rows(group_rows, order, stage)
            copies = []
            for d, (device, place) in enumerate(zip(peers[axis], places[axis])):
                at = pl.ds(pl.multiple_of(starts[g] + place * size, size), size)
                gsend[at, :] = gacc[at, :].astype(BF16)
                copy = remote(gsend.at[at], rbufs[g][stage].at[d],
                              rs_s.at[g, stage, d], rs_r.at[g, stage, d], device)
                copy.start()
                copies.append(copy)
            flying.append(copies)
        b_copies = b_send(stage + 1, peers[ORDERS[0][stage]], b_first[stage])
        for g, order in enumerate(ORDERS):
            axis = order[stage]
            size = part_rows(group_rows, order, stage)
            for copy in flying[g]:
                copy.wait_recv()
            keep = starts[g] + mine[axis] * size
            at = pl.ds(pl.multiple_of(keep, size), size)
            total = gacc[at, :]
            for d in range(len(flying[g])):
                total = total + rbufs[g][stage][d].astype(F32)
            gacc[at, :] = total
            history[g].append(starts[g])
            starts[g] = keep
            sent += flying[g]
        b_sum(stage + 1, b_copies, b_first[stage])
        sent += b_copies
    gb_ref[...] = jnp.sum(bstate[4], axis=0, keepdims=True)

    last = part_rows(group_rows, ORDERS[0], 2)
    for g in range(3):
        at = pl.ds(pl.multiple_of(starts[g], last), last)
        gfin[at, :] = gacc[at, :].astype(BF16)
    for stage in (2, 1, 0):
        flying = []
        for g, order in enumerate(ORDERS):
            axis = order[stage]
            size = part_rows(group_rows, order, stage)
            at = pl.ds(pl.multiple_of(starts[g], size), size)
            for d, device in enumerate(peers[axis]):
                copy = remote(gfin.at[at], gfin.at[at],
                              ag_s.at[g, stage, d], ag_r.at[g, stage, d], device)
                copy.start()
                sent.append(copy)
            for d, place in enumerate(places[axis]):
                there = pl.ds(pl.multiple_of(history[g][stage] + place * size, size), size)
                flying.append(remote(gfin.at[there], gfin.at[there],
                                     ag_s.at[g, stage, d], ag_r.at[g, stage, d], peers[axis][d]))
            starts[g] = history[g][stage]
        for copy in flying:
            copy.wait_recv()
    core_copy.wait_send()
    sent.remove(core_copy)
    final = remote(gfin, gfull_in, fs, fr, other_core)
    final.start()
    gw_ref[:, pl.ds(pl.multiple_of(c * cw, 128), cw)] = gfin[...].astype(F32)
    final.wait_recv()
    gw_ref[:, pl.ds(pl.multiple_of((1 - c) * cw, 128), cw)] = gfull_in[...].astype(F32)
    final.wait_send()

    for i in range(2):
        @pl.when(ups[i])
        def _():
            z_copy(i, everything, zup.at[i], zrecv.at[i, 0], up).wait_send()
        y_copy(i, everything, yrecv.at[i, 0]).wait_send()
        for j in range(2):
            c_copy(i, j, everything).wait_send()

    @pl.when(w == 1)
    def _():
        z_copy(1, everything, zdown.at[0], zrecv.at[1, 0], down).wait_send()
    for t in range(2):
        p_copy(t).wait_send()
    for copy in sent:
        copy.wait_send()


def in_kernel(features, tiles, tile_cols, tile_mask, weight, bias, cotangent):
    rows, width = features.shape
    half = rows // 2
    cw = width // 2
    group_rows = width // 3
    vmem = pl.BlockSpec(memory_space=pltpu.VMEM)
    smem = pl.BlockSpec(memory_space=pltpu.SMEM)
    hbm = pl.BlockSpec(memory_space=pl.ANY)
    dma = pltpu.SemaphoreType.DMA
    rbufs = [
        pltpu.VMEM((WAYS[order[stage]] - 1, part_rows(group_rows, order, stage), cw), BF16)
        for order in ORDERS
        for stage in range(3)
    ]
    out, grad_weight, grad_bias = pl.pallas_call(
        kernel,
        out_shape=(
            jax.ShapeDtypeStruct((half, width), BF16),
            jax.ShapeDtypeStruct((width, width), F32),
            jax.ShapeDtypeStruct((1, width), F32),
        ),
        in_specs=[hbm, hbm, smem, smem, hbm, vmem, hbm],
        out_specs=(vmem, vmem, vmem),
        scratch_shapes=[pltpu.VMEM((rows, width), BF16)] * 8
        + [
            pltpu.VMEM(tiles.shape, BF16),
            pltpu.VMEM(weight.shape, BF16),
            pltpu.VMEM(cotangent.shape, BF16),
            pltpu.VMEM((8, rows, rows), BF16),
            pltpu.VMEM((rows, width), F32),
            pltpu.VMEM((half, width), BF16),
            pltpu.VMEM((half, width), BF16),
            pltpu.VMEM((half, width), BF16),
            pltpu.VMEM((half, width), BF16),
            pltpu.VMEM((width, cw), F32),
            pltpu.VMEM((width, cw), BF16),
            pltpu.VMEM((width, cw), BF16),
            pltpu.VMEM((width, cw), BF16),
            pltpu.VMEM((width, cw), BF16),
            pltpu.VMEM((width, cw), BF16),
        ]
        + rbufs
        + [
            pltpu.VMEM((5, 8, width), F32),
            pltpu.VMEM((6, 8, width), F32),
            dma((4,)), dma((2, CHUNKS)), dma((2, CHUNKS)), dma((4,)),
            dma((2,)), dma((1,)), dma((2,)), dma((4,)),
            dma((2,)), dma((2,)), dma, dma,
            dma((3, 3, 3)), dma((3, 3, 3)), dma((3, 3, 3)), dma((3, 3, 3)),
            dma, dma, dma((6,)), dma((6,)),
        ],
        compiler_params=pltpu.CompilerParams(
            collective_id=0, has_side_effects=True, vmem_limit_bytes=48 * 1024 * 1024
        ),
    )(features, tiles, tile_cols.reshape(-1), tile_mask.reshape(-1), weight, bias.reshape(1, -1), cotangent)
    return out, grad_weight, grad_bias.reshape(-1)


def solution(mesh):
    placed = (
        P("dom", None),
        P("dom", "rep", None, None, None),
        P("dom", "rep", None),
        P("dom", "rep", None),
        P(),
        P(),
        P(("dom", "rep"), None),
    )
    body = in_kernel if (mesh.shape["dom"], mesh.shape["rep"]) == (16, 2) else on_device
    return jax.shard_map(
        body,
        mesh=mesh,
        in_specs=placed,
        out_specs=(P(("dom", "rep"), None), P(), P()),
        check_vma=False,
    )
```

```python
import functools

import jax
import jax.numpy as jnp
from jax import lax
from jax.experimental import pallas as pl
from jax.experimental.pallas import tpu as pltpu
from jax.sharding import PartitionSpec as P

MESH = pl.DeviceIdType.MESH
CHUNKS = 4
THIRDS = 3
F32 = jnp.float32
BF16 = jnp.bfloat16


def spread(value, axis, source):
    kept = jnp.where(lax.axis_index(axis) == source, value, 0).astype(value.dtype)
    return lax.psum(kept, axis)


def section_term(source, tiles, tile_cols, tile_mask, section):
    rblocks = tiles.shape[0]
    tile_side = tiles.shape[3]
    feat_width = source.shape[1]
    source_blocks = source.reshape(source.shape[0] // tile_side, tile_side, feat_width)
    columns = lax.dynamic_index_in_dim(tile_cols, section, 1, keepdims=False)
    live = lax.dynamic_index_in_dim(tile_mask, section, 1, keepdims=False)
    tile_set = lax.dynamic_index_in_dim(tiles, section, 1, keepdims=False)
    block_ids = jnp.arange(source_blocks.shape[0])
    selector = ((columns[:, :, None] == block_ids[None, None, :]) * live[:, :, None]).astype(
        jnp.bfloat16
    )
    picked = jnp.einsum(
        "bkc,cjd->bkjd", selector, source_blocks, preferred_element_type=jnp.float32
    ).astype(jnp.bfloat16)
    summed = jnp.einsum("bkij,bkjd->bid", tile_set, picked, preferred_element_type=jnp.float32)
    return summed.reshape(rblocks * tile_side, feat_width)


def on_device(features, tiles, tile_cols, tile_mask, weight, bias, cotangent):
    sections = tiles.shape[1]
    replica = lax.axis_index("rep")
    aggregate = jnp.zeros(features.shape, jnp.float32)
    for turn_index in range(sections):
        root_index = replica * sections + turn_index
        source = spread(features, "dom", root_index)
        aggregate = aggregate + section_term(source, tiles, tile_cols, tile_mask, turn_index)
    rows_sum = lax.psum_scatter(
        aggregate.astype(jnp.bfloat16), "rep", scatter_dimension=0, tiled=True
    )
    pre_act = jnp.dot(rows_sum, weight, preferred_element_type=jnp.float32) + bias
    sigmoid_pre = jax.nn.sigmoid(pre_act)
    output = (pre_act * sigmoid_pre).astype(jnp.bfloat16)
    grad_pre = cotangent.astype(jnp.float32) * sigmoid_pre * (1.0 + pre_act * (1.0 - sigmoid_pre))
    grad_low = grad_pre.astype(jnp.bfloat16)
    local_weight = jnp.einsum("nd,ne->de", rows_sum, grad_low, preferred_element_type=jnp.float32)
    local_bias = jnp.sum(grad_pre, axis=0)
    grad_weight, grad_bias = lax.psum((local_weight, local_bias), ("dom", "rep"))
    return (output, grad_weight, grad_bias)


ORDERS = (("x", "y", "z"), ("y", "z", "x"), ("z", "x", "y"))
WAYS = {"x": 2, "y": 2, "z": 4}


def part_rows(group_rows, order, stage):
    rows = group_rows
    for axis in order[: stage + 1]:
        rows //= WAYS[axis]
    return rows


def kernel(feat_hbm, tiles_hbm, cols, mask, weight_hbm, bias_ref, cot_hbm,
           out_ref, gw_ref, gb_ref,
           s000, s001, s010, s011, s100, s101, s110, s111,
           tiles_v, weight_v, cot_v, dense, acc,
           part_out, part_in, mixed, pre_acc, glow,
           gacc, gsend, gcore_out, gcore_in, gfin, gfull_in,
           rb00, rb01, rb02, rb10, rb11, rb12, rb20, rb21, rb22,
           bstate, brecv,
           lsem, zrecv, yrecv, crecv, zup, zdown, ysend, csend,
           psend, precv, gcs, gcr, rs_s, rs_r, ag_s, ag_r, fs, fr, bs, br):
    slots = [[[s000, s001], [s010, s011]], [[s100, s101], [s110, s111]]]
    rbufs = [[rb00, rb01, rb02], [rb10, rb11, rb12], [rb20, rb21, rb22]]
    me = lax.axis_index("dom")
    r = lax.axis_index("rep")
    z = lax.div(me, 4)
    y = lax.rem(lax.div(me, 2), 2)
    c = lax.rem(me, 2)
    w = z + r * (3 - 2 * z)
    dz = 1 - 2 * r
    rblocks, sections, ways, side, _ = tiles_v.shape
    _, rows, tw = acc.shape
    width = THIRDS * tw
    crows = rows // CHUNKS
    half = rows // 2

    def dev(zz, yy, cc, rr):
        return (zz * 4 + yy * 2 + cc, rr)

    def z_peer(d):
        z2 = lax.rem(lax.div(z, 2) + d // 2, 2)
        z1 = lax.rem(lax.rem(z, 2) + d % 2, 2)
        return z2 * 2 + z1

    peers = {
        "x": [dev(z, y, c, 1 - r)],
        "y": [dev(z, 1 - y, c, r)],
        "z": [dev(z_peer(d), y, c, r) for d in (1, 2, 3)],
    }
    places = {"x": [1 - r], "y": [1 - y], "z": [z_peer(d) for d in (1, 2, 3)]}
    mine = {"x": r, "y": y, "z": z}
    other_core = dev(z, y, 1 - c, r)
    up = dev(jnp.clip(z + dz, 0, 3), y, c, r)
    down = dev(jnp.clip(z - dz, 0, 3), y, c, r)

    def remote(src, dst, ss, rs, device):
        return pltpu.make_async_remote_copy(
            src_ref=src, dst_ref=dst, send_sem=ss, recv_sem=rs, device_id=device, device_id_type=MESH
        )

    def own_load(i, t):
        return pltpu.make_async_copy(
            feat_hbm.at[:, t * tw:(t + 1) * tw], slots[i][0][0].at[t], lsem.at[3 + t]
        )

    for i in range(2):
        @pl.when(w == i)
        def _():
            for t in range(THIRDS):
                own_load(i, t).start()
    tiles_load = pltpu.make_async_copy(tiles_hbm, tiles_v, lsem.at[0])
    weight_load = pltpu.make_async_copy(weight_hbm, weight_v, lsem.at[1])
    cot_load = pltpu.make_async_copy(cot_hbm, cot_v, lsem.at[2])
    tiles_load.start()
    weight_load.start()
    cot_load.start()
    barrier = pltpu.get_barrier_semaphore()
    greeted = [other_core] + peers["x"] + peers["y"] + peers["z"]
    for device in greeted:
        pl.semaphore_signal(barrier, inc=1, device_id=device, device_id_type=MESH)
    pl.semaphore_wait(barrier, len(greeted))

    everything = pl.ds(0, rows)

    def chunk(ch):
        return pl.ds(pl.multiple_of(ch * crows, crows), crows)

    def z_copy(t, i, at, sem, rsem, device):
        slot = slots[i][0][0]
        return remote(slot.at[t, at], slot.at[t, at], sem, rsem, device)

    def y_copy(t, i, at, rsem):
        return remote(slots[i][0][0].at[t, at], slots[i][1][0].at[t, at],
                      ysend.at[t, i], rsem, peers["y"][0])

    def c_copy(t, i, j, at):
        return remote(slots[i][j][0].at[t, at], slots[i][j][1].at[t, at],
                      csend.at[t, 2 * i + j], crecv.at[t, 2 * i + j], other_core)

    ups = {0: w <= 2, 1: jnp.logical_and(w >= 1, w <= 2)}

    def forward(t, i, ch):
        at = chunk(ch)

        @pl.when(ups[i])
        def _():
            z_copy(t, i, at, zup.at[t, i], zrecv.at[t, i, ch], up).start()

        if i == 1:
            @pl.when(w == 1)
            def _():
                z_copy(t, i, at, zdown.at[t], zrecv.at[t, i, ch], down).start()
        y_copy(t, i, at, yrecv.at[t, i, ch]).start()
        c_copy(t, i, 0, at).start()

    def up_sent(t, i):
        z_copy(t, i, everything, zup.at[t, i], zrecv.at[t, i, 0], up).wait_send()

    def own_step(t):
        for i in range(2):
            @pl.when(w == i)
            def _():
                own_load(i, t).wait()
                if t > 0:
                    up_sent(t - 1, i)

                @pl.loop(0, CHUNKS)
                def _(ch):
                    forward(t, i, ch)

    def z_step(t, i, ch):
        @pl.when(w != i)
        def _():
            z_copy(t, i, chunk(ch), zup.at[t, i], zrecv.at[t, i, ch], up).wait_recv()
            forward(t, i, ch)

    def y_step(t, i, ch):
        y_copy(t, i, chunk(ch), yrecv.at[t, i, ch]).wait_recv()
        c_copy(t, i, 1, chunk(ch)).start()

    def assemble(index):
        i = 1 - lax.div(index, 4)
        j = lax.rem(lax.div(index, 2), 2)
        k = lax.rem(index, 2)
        zz = i + r * (1 - 2 * i)
        section = zz * 4 + (y + j - 2 * y * j) * 2 + (c + k - 2 * c * k)

        @pl.loop(0, rblocks)
        def _(b):
            tile_of = [tiles_v[b, section, t].astype(F32) for t in range(ways)]
            for block in range(rows // side):
                total = None
                for t in range(ways):
                    take = jnp.logical_and(cols[b, t, section] == block, mask[b, t, section] != 0)
                    term = tile_of[t] * jnp.where(take, 1.0, 0.0)
                    total = term if total is None else total + term
                dense[index, pl.ds(pl.multiple_of(b * side, side), side),
                      block * side:(block + 1) * side] = total.astype(BF16)

    def product(t, i, j, k, at):
        index = (1 - i) * 4 + j * 2 + k
        return jnp.dot(dense[index, at, :], slots[i][j][k][t], preferred_element_type=F32)

    def add_product(t, i, j, k):
        if k == 1:
            c_copy(t, i, j, everything).wait_recv()
        term = product(t, i, j, k, everything)
        if (i, j, k) == (1, 0, 0):
            acc[t] = term
        else:
            acc[t] = acc[t] + term

    def p_copy(t):
        return remote(part_out.at[t], part_in.at[t], psend.at[t], precv.at[t], peers["x"][0])

    peer_rows = pl.ds(pl.multiple_of((1 - r) * half, half), half)
    own_rows = pl.ds(pl.multiple_of(r * half, half), half)

    def exchange(t):
        part_out[t] = acc[t, peer_rows, :].astype(BF16)
        p_copy(t).start()
        mixed[t] = acc[t, own_rows, :].astype(BF16)

    def meet(t):
        p_copy(t).wait_recv()
        low = (mixed[t].astype(F32) + part_in[t].astype(F32)).astype(BF16)
        mixed[t] = low
        return jnp.dot(low, weight_v[t * tw:(t + 1) * tw, :], preferred_element_type=F32)

    jobs = [(i, j, k) for i in (1, 0) for j in range(2) for k in range(2)]
    order = [(t, i, ch) for t in range(THIRDS) for i in (1, 0) for ch in range(CHUNKS)]
    lag = 2
    for position, (t, i, ch) in enumerate(order):
        if i == 1 and ch == 0:
            own_step(t)
        if position == 0:
            tiles_load.wait()
        z_step(t, i, ch)
        if position >= lag:
            y_step(*order[position - lag])
        step = position % (2 * CHUNKS)
        if t == 0:
            assemble(step)
        elif t < THIRDS - 1:
            add_product(t - 1, *jobs[step])
            if step == 7:
                exchange(t - 1)
        elif step < 4:
            add_product(t - 1, *jobs[2 * step])
            add_product(t - 1, *jobs[2 * step + 1])
            if step == 3:
                exchange(t - 1)
        else:
            if step == 5:
                weight_load.wait()
                pre_acc[...] = meet(0) + bias_ref[...].reshape(1, width)
            add_product(t, *jobs[step - 4])
    for behind in range(lag, 0, -1):
        y_step(*order[-behind])
    last_third = THIRDS - 1
    c_copy(last_third, 0, 0, everything).wait_recv()
    c_copy(last_third, 0, 1, everything).wait_recv()

    def finish(at, target):
        total = acc[last_third, at, :]
        for j in range(2):
            for k in range(2):
                total = total + product(last_third, 0, j, k, at)
        target[last_third] = total.astype(BF16)

    finish(peer_rows, part_out)
    p_copy(last_third).start()
    finish(own_rows, mixed)
    for t in range(1, last_third):
        pre_acc[...] = pre_acc[...] + meet(t)
    cot_load.wait()
    pre = pre_acc[...] + meet(last_third)
    sig = 1.0 / (1.0 + jnp.exp(-pre))
    out_ref[...] = (pre * sig).astype(BF16)
    grad = cot_v[...].astype(F32) * sig * (1.0 + pre * (1.0 - sig))
    glow[...] = grad.astype(BF16)
    bias_rows = jnp.sum(grad.reshape(half // 8, 8, width), axis=0)

    cw = width // 2
    group_rows = tw

    def grad_part(g, start):
        lanes = pl.ds(pl.multiple_of(start, 128), cw)
        return lax.dot_general(mixed[g], glow[:, lanes], (((0,), (0,)), ((), ())),
                               preferred_element_type=F32)

    def b_send(stage, axis_peers, first):
        copies = []
        for d, device in enumerate(axis_peers):
            copies.append(remote(bstate.at[stage], brecv.at[first + d], bs.at[first + d],
                                 br.at[first + d], device))
            copies[-1].start()
        return copies

    def b_sum(stage, copies, first):
        for copy in copies:
            copy.wait_recv()
        total = bstate[stage] + brecv[first]
        if len(copies) == 3:
            total = total + (brecv[first + 1] + brecv[first + 2])
        bstate[stage + 1] = total

    sent = []
    bstate[0] = bias_rows
    core_copies = []
    for g in range(3):
        at = pl.ds(g * group_rows, group_rows)
        gcore_out[at, :] = grad_part(g, (1 - c) * cw).astype(BF16)
        core_copies.append(remote(gcore_out.at[at], gcore_in.at[at], gcs.at[g], gcr.at[g], other_core))
        core_copies[-1].start()
    b_copies = b_send(0, [other_core], 0)
    sent += core_copies + b_copies
    for g in range(3):
        gacc[pl.ds(g * group_rows, group_rows), :] = grad_part(g, c * cw)

    starts = [g * group_rows for g in range(3)]
    history = [[], [], []]
    flying = [None, None, None]

    def scatter(g, stage):
        axis = ORDERS[g][stage]
        size = part_rows(group_rows, ORDERS[g], stage)
        copies = []
        for d, (device, place) in enumerate(zip(peers[axis], places[axis])):
            at = pl.ds(pl.multiple_of(starts[g] + place * size, size), size)
            gsend[at, :] = gacc[at, :].astype(BF16)
            copies.append(remote(gsend.at[at], rbufs[g][stage].at[d],
                                 rs_s.at[g, stage, d], rs_r.at[g, stage, d], device))
            copies[-1].start()
        flying[g] = copies
        sent.extend(copies)

    def gather(g, stage):
        axis = ORDERS[g][stage]
        size = part_rows(group_rows, ORDERS[g], stage)
        at = pl.ds(pl.multiple_of(starts[g], size), size)
        arriving = []
        for d, (device, place) in enumerate(zip(peers[axis], places[axis])):
            copy = remote(gfin.at[at], gfin.at[at], ag_s.at[g, stage, d], ag_r.at[g, stage, d], device)
            copy.start()
            sent.append(copy)
            there = pl.ds(pl.multiple_of(history[g][stage] + place * size, size), size)
            arriving.append((there, remote(gfin.at[there], gfin.at[there], ag_s.at[g, stage, d],
                                           ag_r.at[g, stage, d], device)))
        starts[g] = history[g][stage]
        flying[g] = arriving

    def to_core(at):
        remote(gfin.at[at], gfull_in.at[at], fs, fr, other_core).start()

    for g in range(3):
        at = pl.ds(g * group_rows, group_rows)
        core_copies[g].wait_recv()
        gacc[at, :] = gacc[at, :] + gcore_in[at, :].astype(F32)
        scatter(g, 0)
    b_sum(0, b_copies, 0)
    b_first = (1, 2, 3)
    for stage in range(3):
        b_copies = b_send(stage + 1, peers[ORDERS[0][stage]], b_first[stage])
        sent += b_copies
        for g, order_g in enumerate(ORDERS):
            size = part_rows(group_rows, order_g, stage)
            for copy in flying[g]:
                copy.wait_recv()
            keep = starts[g] + mine[order_g[stage]] * size
            at = pl.ds(pl.multiple_of(keep, size), size)
            total = gacc[at, :]
            for d in range(len(flying[g])):
                total = total + rbufs[g][stage][d].astype(F32)
            history[g].append(starts[g])
            starts[g] = keep
            if stage < 2:
                gacc[at, :] = total
                scatter(g, stage + 1)
            else:
                gfin[at, :] = total.astype(BF16)
                gather(g, 2)
                to_core(at)
        b_sum(stage + 1, b_copies, b_first[stage])
    for stage in (2, 1, 0):
        for g in range(3):
            arriving = flying[g]
            for _, copy in arriving:
                copy.wait_recv()
            if stage > 0:
                gather(g, stage - 1)
            for there, _ in arriving:
                to_core(there)
    gb_ref[...] = jnp.sum(bstate[4], axis=0)
    gw_ref[:, pl.ds(pl.multiple_of(c * cw, 128), cw)] = gfin[...].astype(F32)
    final = remote(gfin, gfull_in, fs, fr, other_core)
    final.wait_recv()
    gw_ref[:, pl.ds(pl.multiple_of((1 - c) * cw, 128), cw)] = gfull_in[...].astype(F32)
    final.wait_send()

    for t in range(THIRDS):
        for i in range(2):
            waited = w != i if t < THIRDS - 1 else w >= 0

            @pl.when(jnp.logical_and(ups[i], waited))
            def _():
                up_sent(t, i)
            y_copy(t, i, everything, yrecv.at[t, i, 0]).wait_send()
            for j in range(2):
                c_copy(t, i, j, everything).wait_send()

        @pl.when(w == 1)
        def _():
            z_copy(t, 1, everything, zdown.at[t], zrecv.at[t, 1, 0], down).wait_send()
        p_copy(t).wait_send()
    for copy in sent:
        copy.wait_send()


def in_kernel(features, tiles, tile_cols, tile_mask, weight, bias, cotangent):
    rows, width = features.shape
    half = rows // 2
    cw = width // 2
    tw = width // THIRDS
    vmem = pl.BlockSpec(memory_space=pltpu.VMEM)
    smem = pl.BlockSpec(memory_space=pltpu.SMEM)
    hbm = pl.BlockSpec(memory_space=pltpu.HBM)
    dma = pltpu.SemaphoreType.DMA
    rbufs = [
        pltpu.VMEM((WAYS[order[stage]] - 1, part_rows(tw, order, stage), cw), BF16)
        for order in ORDERS
        for stage in range(3)
    ]
    return pl.pallas_call(
        kernel,
        out_shape=(
            jax.ShapeDtypeStruct((half, width), BF16),
            jax.ShapeDtypeStruct((width, width), F32),
            jax.ShapeDtypeStruct((width,), F32),
        ),
        in_specs=[hbm, hbm, smem, smem, hbm, vmem, hbm],
        out_specs=(vmem, vmem, vmem),
        scratch_shapes=[pltpu.VMEM((THIRDS, rows, tw), BF16)] * 8
        + [
            pltpu.VMEM(tiles.shape, BF16),
            pltpu.VMEM(weight.shape, BF16),
            pltpu.VMEM(cotangent.shape, BF16),
            pltpu.VMEM((8, rows, rows), BF16),
            pltpu.VMEM((THIRDS, rows, tw), F32),
            pltpu.VMEM((THIRDS, half, tw), BF16),
            pltpu.VMEM((THIRDS, half, tw), BF16),
            pltpu.VMEM((THIRDS, half, tw), BF16),
            pltpu.VMEM((half, width), F32),
            pltpu.VMEM((half, width), BF16),
            pltpu.VMEM((width, cw), F32),
        ]
        + [pltpu.VMEM((width, cw), BF16)] * 5
        + rbufs
        + [
            pltpu.VMEM((5, 8, width), F32),
            pltpu.VMEM((6, 8, width), F32),
            dma((3 + THIRDS,)), dma((THIRDS, 2, CHUNKS)), dma((THIRDS, 2, CHUNKS)), dma((THIRDS, 4)),
            dma((THIRDS, 2)), dma((THIRDS,)), dma((THIRDS, 2)), dma((THIRDS, 4)),
            dma((THIRDS,)), dma((THIRDS,)), dma((3,)), dma((3,)),
            dma((3, 3, 3)), dma((3, 3, 3)), dma((3, 3, 3)), dma((3, 3, 3)),
            dma, dma, dma((6,)), dma((6,)),
        ],
        compiler_params=pltpu.CompilerParams(
            collective_id=0, has_side_effects=True, vmem_limit_bytes=48 * 1024 * 1024
        ),
    )(features, tiles, tile_cols.transpose(0, 2, 1), tile_mask.transpose(0, 2, 1), weight, bias, cotangent)


def solution(mesh):
    placed = (
        P("dom", None),
        P("dom", "rep", None, None, None),
        P("dom", "rep", None),
        P("dom", "rep", None),
        P(),
        P(),
        P(("dom", "rep"), None),
    )
    body = in_kernel if (mesh.shape["dom"], mesh.shape["rep"]) == (16, 2) else on_device
    return jax.shard_map(
        body,
        mesh=mesh,
        in_specs=placed,
        out_specs=(P(("dom", "rep"), None), P(), P()),
        check_vma=False,
    )
```

```python
import functools

import jax
import jax.numpy as jnp
from jax import lax
from jax.experimental import pallas as pl
from jax.experimental.pallas import tpu as pltpu
from jax.sharding import PartitionSpec as P

MESH = pl.DeviceIdType.MESH
CHUNKS = 4
THIRDS = 3
F32 = jnp.float32
BF16 = jnp.bfloat16


def spread(value, axis, source):
    kept = jnp.where(lax.axis_index(axis) == source, value, 0).astype(value.dtype)
    return lax.psum(kept, axis)


def section_term(source, tiles, tile_cols, tile_mask, section):
    rblocks = tiles.shape[0]
    tile_side = tiles.shape[3]
    feat_width = source.shape[1]
    source_blocks = source.reshape(source.shape[0] // tile_side, tile_side, feat_width)
    columns = lax.dynamic_index_in_dim(tile_cols, section, 1, keepdims=False)
    live = lax.dynamic_index_in_dim(tile_mask, section, 1, keepdims=False)
    tile_set = lax.dynamic_index_in_dim(tiles, section, 1, keepdims=False)
    block_ids = jnp.arange(source_blocks.shape[0])
    selector = ((columns[:, :, None] == block_ids[None, None, :]) * live[:, :, None]).astype(
        jnp.bfloat16
    )
    picked = jnp.einsum(
        "bkc,cjd->bkjd", selector, source_blocks, preferred_element_type=jnp.float32
    ).astype(jnp.bfloat16)
    summed = jnp.einsum("bkij,bkjd->bid", tile_set, picked, preferred_element_type=jnp.float32)
    return summed.reshape(rblocks * tile_side, feat_width)


def on_device(features, tiles, tile_cols, tile_mask, weight, bias, cotangent):
    sections = tiles.shape[1]
    replica = lax.axis_index("rep")
    aggregate = jnp.zeros(features.shape, jnp.float32)
    for turn_index in range(sections):
        root_index = replica * sections + turn_index
        source = spread(features, "dom", root_index)
        aggregate = aggregate + section_term(source, tiles, tile_cols, tile_mask, turn_index)
    rows_sum = lax.psum_scatter(
        aggregate.astype(jnp.bfloat16), "rep", scatter_dimension=0, tiled=True
    )
    pre_act = jnp.dot(rows_sum, weight, preferred_element_type=jnp.float32) + bias
    sigmoid_pre = jax.nn.sigmoid(pre_act)
    output = (pre_act * sigmoid_pre).astype(jnp.bfloat16)
    grad_pre = cotangent.astype(jnp.float32) * sigmoid_pre * (1.0 + pre_act * (1.0 - sigmoid_pre))
    grad_low = grad_pre.astype(jnp.bfloat16)
    local_weight = jnp.einsum("nd,ne->de", rows_sum, grad_low, preferred_element_type=jnp.float32)
    local_bias = jnp.sum(grad_pre, axis=0)
    grad_weight, grad_bias = lax.psum((local_weight, local_bias), ("dom", "rep"))
    return (output, grad_weight, grad_bias)


ORDERS = (("x", "y", "z"), ("y", "z", "x"), ("z", "x", "y"))
WAYS = {"x": 2, "y": 2, "z": 4}


def part_rows(group_rows, order, stage):
    rows = group_rows
    for axis in order[: stage + 1]:
        rows //= WAYS[axis]
    return rows


def kernel(feat_hbm, tiles_hbm, cols_hbm, mask_hbm, weight_hbm, bias_hbm, cot_hbm,
           out_ref, gw_ref, gb_ref,
           s000, s001, s010, s011, s100, s101, s110, s111,
           tiles_v, weight_v, cot_v, cols, mask, bias_ref, dense, acc,
           part_out, part_in, mixed, mixed_t, pre_acc, glow,
           gacc, gsend, gcore_out, gcore_in,
           rb00, rb01, rb02, rb10, rb11, rb12, rb20, rb21, rb22,
           bstate, brecv,
           lsem, zrecv, yrecv, crecv, zup, zdown, ysend, csend,
           psend, precv, gcs, gcr, rs_s, rs_r, ag_s, ag_r, fs, fr, bs, br):
    slots = [[[s000, s001], [s010, s011]], [[s100, s101], [s110, s111]]]
    rbufs = [[rb00, rb01, rb02], [rb10, rb11, rb12], [rb20, rb21, rb22]]
    me = lax.axis_index("dom")
    r = lax.axis_index("rep")
    z = lax.div(me, 4)
    y = lax.rem(lax.div(me, 2), 2)
    c = lax.rem(me, 2)
    w = z + r * (3 - 2 * z)
    dz = 1 - 2 * r
    rblocks, sections, ways, side, _ = tiles_v.shape
    _, rows, tw = acc.shape
    width = THIRDS * tw
    crows = rows // CHUNKS
    half = rows // 2

    def dev(zz, yy, cc, rr):
        return (zz * 4 + yy * 2 + cc, rr)

    def z_peer(d):
        z2 = lax.rem(lax.div(z, 2) + d // 2, 2)
        z1 = lax.rem(lax.rem(z, 2) + d % 2, 2)
        return z2 * 2 + z1

    peers = {
        "x": [dev(z, y, c, 1 - r)],
        "y": [dev(z, 1 - y, c, r)],
        "z": [dev(z_peer(d), y, c, r) for d in (1, 2, 3)],
    }
    places = {"x": [1 - r], "y": [1 - y], "z": [z_peer(d) for d in (1, 2, 3)]}
    mine = {"x": r, "y": y, "z": z}
    other_core = dev(z, y, 1 - c, r)
    up = dev(jnp.clip(z + dz, 0, 3), y, c, r)
    down = dev(jnp.clip(z - dz, 0, 3), y, c, r)

    def remote(src, dst, ss, rs, device):
        return pltpu.make_async_remote_copy(
            src_ref=src, dst_ref=dst, send_sem=ss, recv_sem=rs, device_id=device, device_id_type=MESH
        )

    def own_load(i, t):
        return pltpu.make_async_copy(
            feat_hbm.at[:, t * tw:(t + 1) * tw], slots[i][0][0].at[t], lsem.at[6 + t]
        )

    for i in range(2):
        @pl.when(w == i)
        def _():
            for t in range(THIRDS):
                own_load(i, t).start()
    tiles_load = pltpu.make_async_copy(tiles_hbm, tiles_v, lsem.at[0])
    weight_load = pltpu.make_async_copy(weight_hbm, weight_v, lsem.at[1])
    cot_load = pltpu.make_async_copy(cot_hbm, cot_v, lsem.at[2])
    cols_load = pltpu.make_async_copy(cols_hbm, cols, lsem.at[3])
    mask_load = pltpu.make_async_copy(mask_hbm, mask, lsem.at[4])
    bias_load = pltpu.make_async_copy(bias_hbm, bias_ref, lsem.at[5])
    cols_load.start()
    mask_load.start()
    bias_load.start()
    tiles_load.start()
    weight_load.start()
    cot_load.start()
    barrier = pltpu.get_barrier_semaphore()
    greeted = [other_core] + peers["x"] + peers["y"] + peers["z"]
    for device in greeted:
        pl.semaphore_signal(barrier, inc=1, device_id=device, device_id_type=MESH)
    pl.semaphore_wait(barrier, len(greeted))

    everything = pl.ds(0, rows)

    def chunk(ch):
        return pl.ds(pl.multiple_of(ch * crows, crows), crows)

    def z_copy(t, i, at, sem, rsem, device):
        slot = slots[i][0][0]
        return remote(slot.at[t, at], slot.at[t, at], sem, rsem, device)

    def y_copy(t, i, at, rsem):
        return remote(slots[i][0][0].at[t, at], slots[i][1][0].at[t, at],
                      ysend.at[t, i], rsem, peers["y"][0])

    def c_copy(t, i, j, at):
        return remote(slots[i][j][0].at[t, at], slots[i][j][1].at[t, at],
                      csend.at[t, 2 * i + j], crecv.at[t, 2 * i + j], other_core)

    ups = {0: w <= 2, 1: jnp.logical_and(w >= 1, w <= 2)}

    def forward(t, i, ch):
        at = chunk(ch)

        @pl.when(ups[i])
        def _():
            z_copy(t, i, at, zup.at[t, i], zrecv.at[t, i, ch], up).start()

        if i == 1:
            @pl.when(w == 1)
            def _():
                z_copy(t, i, at, zdown.at[t], zrecv.at[t, i, ch], down).start()
        y_copy(t, i, at, yrecv.at[t, i, ch]).start()
        c_copy(t, i, 0, at).start()

    def up_sent(t, i):
        z_copy(t, i, everything, zup.at[t, i], zrecv.at[t, i, 0], up).wait_send()

    def own_step(t):
        for i in range(2):
            @pl.when(w == i)
            def _():
                own_load(i, t).wait()
                if t > 0:
                    up_sent(t - 1, i)

                @pl.loop(0, CHUNKS)
                def _(ch):
                    forward(t, i, ch)

    def z_step(t, i, ch):
        @pl.when(w != i)
        def _():
            z_copy(t, i, chunk(ch), zup.at[t, i], zrecv.at[t, i, ch], up).wait_recv()
            forward(t, i, ch)

    def y_step(t, i, ch):
        y_copy(t, i, chunk(ch), yrecv.at[t, i, ch]).wait_recv()
        c_copy(t, i, 1, chunk(ch)).start()

    def assemble(index):
        i = 1 - lax.div(index, 4)
        j = lax.rem(lax.div(index, 2), 2)
        k = lax.rem(index, 2)
        zz = i + r * (1 - 2 * i)
        section = zz * 4 + (y + j - 2 * y * j) * 2 + (c + k - 2 * c * k)

        @pl.loop(0, rblocks)
        def _(b):
            tile_of = [tiles_v[b, section, t].astype(F32) for t in range(ways)]
            for block in range(rows // side):
                total = None
                for t in range(ways):
                    take = jnp.logical_and(cols[b, t, section] == block, mask[b, t, section] != 0)
                    term = tile_of[t] * jnp.where(take, 1.0, 0.0)
                    total = term if total is None else total + term
                dense[index, pl.ds(pl.multiple_of(b * side, side), side),
                      block * side:(block + 1) * side] = total.astype(BF16)

    def product(t, i, j, k, at):
        index = (1 - i) * 4 + j * 2 + k
        return jnp.dot(dense[index, at, :], slots[i][j][k][t], preferred_element_type=F32)

    def add_product(t, i, j, k):
        if k == 1:
            c_copy(t, i, j, everything).wait_recv()
        term = product(t, i, j, k, everything)
        if (i, j, k) == (1, 0, 0):
            acc[t] = term
        else:
            acc[t] = acc[t] + term

    def p_copy(t):
        return remote(part_out.at[t], part_in.at[t], psend.at[t], precv.at[t], peers["x"][0])

    peer_rows = pl.ds(pl.multiple_of((1 - r) * half, half), half)
    own_rows = pl.ds(pl.multiple_of(r * half, half), half)

    def exchange(t):
        part_out[t] = acc[t, peer_rows, :].astype(BF16)
        p_copy(t).start()
        mixed[t] = acc[t, own_rows, :].astype(BF16)

    def meet(t):
        p_copy(t).wait_recv()
        low = (mixed[t].astype(F32) + part_in[t].astype(F32)).astype(BF16)
        mixed[t] = low
        return jnp.dot(low, weight_v[t * tw:(t + 1) * tw, :], preferred_element_type=F32)

    jobs = [(i, j, k) for i in (1, 0) for j in range(2) for k in range(2)]
    order = [(t, i, ch) for t in range(THIRDS) for i in (1, 0) for ch in range(CHUNKS)]
    lag = 2
    for position, (t, i, ch) in enumerate(order):
        if i == 1 and ch == 0:
            own_step(t)
        if position == 0:
            cols_load.wait()
            mask_load.wait()
            tiles_load.wait()
        z_step(t, i, ch)
        if position >= lag:
            y_step(*order[position - lag])
        step = position % (2 * CHUNKS)
        if t == 0:
            assemble(step)
        elif t < THIRDS - 1:
            add_product(t - 1, *jobs[step])
            if step == 7:
                exchange(t - 1)
        elif step < 4:
            add_product(t - 1, *jobs[2 * step])
            add_product(t - 1, *jobs[2 * step + 1])
            if step == 3:
                exchange(t - 1)
        else:
            if step == 5:
                weight_load.wait()
                bias_load.wait()
                pre_acc[...] = meet(0) + bias_ref[...].reshape(1, width)
            add_product(t, *jobs[step - 4])
    for behind in range(lag, 0, -1):
        y_step(*order[-behind])
    last_third = THIRDS - 1
    for t in range(1, last_third):
        pre_acc[...] = pre_acc[...] + meet(t)
    c_copy(last_third, 0, 0, everything).wait_recv()
    c_copy(last_third, 0, 1, everything).wait_recv()

    def finish(at, target):
        total = acc[last_third, at, :]
        for j in range(2):
            for k in range(2):
                total = total + product(last_third, 0, j, k, at)
        target[last_third] = total.astype(BF16)

    finish(peer_rows, part_out)
    p_copy(last_third).start()
    finish(own_rows, mixed)
    for t in range(last_third):
        mixed_t[t] = mixed[t].T
    cot_load.wait()
    pre = pre_acc[...] + meet(last_third)
    mixed_t[last_third] = mixed[last_third].T
    sig = 1.0 / (1.0 + jnp.exp(-pre))
    out_ref[...] = (pre * sig).astype(BF16)
    grad = cot_v[...].astype(F32) * sig * (1.0 + pre * (1.0 - sig))
    glow[...] = grad.astype(BF16)
    bias_rows = jnp.sum(grad.reshape(half // 8, 8, width), axis=0)

    cw = width // 2
    group_rows = tw
    own_cols = pl.ds(pl.multiple_of(c * cw, 128), cw)
    other_cols = pl.ds(pl.multiple_of((1 - c) * cw, 128), cw)

    def grad_part(g, start):
        lanes = pl.ds(pl.multiple_of(start, 128), cw)
        return jnp.dot(mixed_t[g], glow[:, lanes], preferred_element_type=F32)

    def b_send(stage, axis_peers, first):
        copies = []
        for d, device in enumerate(axis_peers):
            copies.append(remote(bstate.at[stage], brecv.at[first + d], bs.at[first + d],
                                 br.at[first + d], device))
            copies[-1].start()
        return copies

    def b_sum(stage, copies, first):
        for copy in copies:
            copy.wait_recv()
        total = bstate[stage] + brecv[first]
        if len(copies) == 3:
            total = total + (brecv[first + 1] + brecv[first + 2])
        bstate[stage + 1] = total

    sent = []
    bstate[0] = bias_rows
    core_copies = []
    for g in range(3):
        at = pl.ds(g * group_rows, group_rows)
        gcore_out[at, :] = grad_part(g, (1 - c) * cw).astype(BF16)
        core_copies.append(remote(gcore_out.at[at], gcore_in.at[at], gcs.at[g], gcr.at[g], other_core))
        core_copies[-1].start()
    b_copies = b_send(0, [other_core], 0)
    sent += core_copies + b_copies
    for g in range(3):
        gacc[pl.ds(g * group_rows, group_rows), :] = grad_part(g, c * cw)

    starts = [g * group_rows for g in range(3)]
    history = [[], [], []]
    flying = [None, None, None]

    def scatter(g, stage):
        axis = ORDERS[g][stage]
        size = part_rows(group_rows, ORDERS[g], stage)
        copies = []
        for d, (device, place) in enumerate(zip(peers[axis], places[axis])):
            at = pl.ds(pl.multiple_of(starts[g] + place * size, size), size)
            gsend[at, :] = gacc[at, :].astype(BF16)
            copies.append(remote(gsend.at[at], rbufs[g][stage].at[d],
                                 rs_s.at[g, stage, d], rs_r.at[g, stage, d], device))
            copies[-1].start()
        flying[g] = copies
        sent.extend(copies)

    def gather(g, stage):
        axis = ORDERS[g][stage]
        size = part_rows(group_rows, ORDERS[g], stage)
        at = pl.ds(pl.multiple_of(starts[g], size), size)
        arriving = []
        for d, (device, place) in enumerate(zip(peers[axis], places[axis])):
            copy = remote(gw_ref.at[at, own_cols], gw_ref.at[at, own_cols], ag_s.at[g, stage, d], ag_r.at[g, stage, d], device)
            copy.start()
            sent.append(copy)
            there = pl.ds(pl.multiple_of(history[g][stage] + place * size, size), size)
            arriving.append((there, remote(gw_ref.at[there, own_cols], gw_ref.at[there, own_cols], ag_s.at[g, stage, d],
                                           ag_r.at[g, stage, d], device)))
        starts[g] = history[g][stage]
        flying[g] = arriving

    def to_core(at):
        remote(gw_ref.at[at, own_cols], gw_ref.at[at, own_cols], fs, fr, other_core).start()

    for g in range(3):
        at = pl.ds(g * group_rows, group_rows)
        core_copies[g].wait_recv()
        gacc[at, :] = gacc[at, :] + gcore_in[at, :].astype(F32)
        scatter(g, 0)
    b_sum(0, b_copies, 0)
    b_first = (1, 2, 3)
    for stage in range(3):
        b_copies = b_send(stage + 1, peers[ORDERS[0][stage]], b_first[stage])
        sent += b_copies
        for g, order_g in enumerate(ORDERS):
            size = part_rows(group_rows, order_g, stage)
            for copy in flying[g]:
                copy.wait_recv()
            keep = starts[g] + mine[order_g[stage]] * size
            at = pl.ds(pl.multiple_of(keep, size), size)
            total = gacc[at, :]
            for d in range(len(flying[g])):
                total = total + rbufs[g][stage][d].astype(F32)
            history[g].append(starts[g])
            starts[g] = keep
            if stage < 2:
                gacc[at, :] = total
                scatter(g, stage + 1)
            else:
                gw_ref[at, own_cols] = total.astype(BF16)
                gather(g, 2)
                to_core(at)
        b_sum(stage + 1, b_copies, b_first[stage])
    for stage in (2, 1, 0):
        for g in range(3):
            arriving = flying[g]
            for _, copy in arriving:
                copy.wait_recv()
            if stage > 0:
                gather(g, stage - 1)
            for there, _ in arriving:
                to_core(there)
    gb_ref[...] = jnp.sum(bstate[4], axis=0)
    remote(gw_ref.at[:, other_cols], gw_ref.at[:, other_cols], fs, fr, other_core).wait_recv()
    remote(gw_ref.at[:, own_cols], gw_ref.at[:, own_cols], fs, fr, other_core).wait_send()

    for t in range(THIRDS):
        for i in range(2):
            waited = w != i if t < THIRDS - 1 else w >= 0

            @pl.when(jnp.logical_and(ups[i], waited))
            def _():
                up_sent(t, i)
            y_copy(t, i, everything, yrecv.at[t, i, 0]).wait_send()
            for j in range(2):
                c_copy(t, i, j, everything).wait_send()

        @pl.when(w == 1)
        def _():
            z_copy(t, 1, everything, zdown.at[t], zrecv.at[t, 1, 0], down).wait_send()
        p_copy(t).wait_send()
    for copy in sent:
        copy.wait_send()


def in_kernel(features, tiles, tile_cols, tile_mask, weight, bias, cotangent):
    rows, width = features.shape
    half = rows // 2
    cw = width // 2
    tw = width // THIRDS
    vmem = pl.BlockSpec(memory_space=pltpu.VMEM)
    hbm = pl.BlockSpec(memory_space=pltpu.HBM)
    dma = pltpu.SemaphoreType.DMA
    rbufs = [
        pltpu.VMEM((WAYS[order[stage]] - 1, part_rows(tw, order, stage), cw), BF16)
        for order in ORDERS
        for stage in range(3)
    ]
    out, grad_weight, grad_bias = pl.pallas_call(
        kernel,
        out_shape=(
            jax.ShapeDtypeStruct((half, width), BF16),
            jax.ShapeDtypeStruct((width, width), BF16),
            jax.ShapeDtypeStruct((width,), F32),
        ),
        in_specs=[hbm] * 7,
        out_specs=(vmem, vmem, vmem),
        scratch_shapes=[pltpu.VMEM((THIRDS, rows, tw), BF16)] * 8
        + [
            pltpu.VMEM(tiles.shape, BF16),
            pltpu.VMEM(weight.shape, BF16),
            pltpu.VMEM(cotangent.shape, BF16),
            pltpu.SMEM((tiles.shape[0], tiles.shape[2], tiles.shape[1]), jnp.int32),
            pltpu.SMEM((tiles.shape[0], tiles.shape[2], tiles.shape[1]), jnp.int32),
            pltpu.VMEM((width,), F32),
            pltpu.VMEM((8, rows, rows), BF16),
            pltpu.VMEM((THIRDS, rows, tw), F32),
            pltpu.VMEM((THIRDS, half, tw), BF16),
            pltpu.VMEM((THIRDS, half, tw), BF16),
            pltpu.VMEM((THIRDS, half, tw), BF16),
            pltpu.VMEM((THIRDS, tw, half), BF16),
            pltpu.VMEM((half, width), F32),
            pltpu.VMEM((half, width), BF16),
            pltpu.VMEM((width, cw), F32),
        ]
        + [pltpu.VMEM((width, cw), BF16)] * 3
        + rbufs
        + [
            pltpu.VMEM((5, 8, width), F32),
            pltpu.VMEM((6, 8, width), F32),
            dma((6 + THIRDS,)), dma((THIRDS, 2, CHUNKS)), dma((THIRDS, 2, CHUNKS)), dma((THIRDS, 4)),
            dma((THIRDS, 2)), dma((THIRDS,)), dma((THIRDS, 2)), dma((THIRDS, 4)),
            dma((THIRDS,)), dma((THIRDS,)), dma((3,)), dma((3,)),
            dma((3, 3, 3)), dma((3, 3, 3)), dma((3, 3, 3)), dma((3, 3, 3)),
            dma, dma, dma((6,)), dma((6,)),
        ],
        compiler_params=pltpu.CompilerParams(
            collective_id=0, has_side_effects=True, vmem_limit_bytes=63 * 1024 * 1024
        ),
    )(features, tiles, tile_cols.transpose(0, 2, 1), tile_mask.transpose(0, 2, 1), weight, bias, cotangent)
    return out, grad_weight.astype(F32), grad_bias


def solution(mesh):
    placed = (
        P("dom", None),
        P("dom", "rep", None, None, None),
        P("dom", "rep", None),
        P("dom", "rep", None),
        P(),
        P(),
        P(("dom", "rep"), None),
    )
    body = in_kernel if (mesh.shape["dom"], mesh.shape["rep"]) == (16, 2) else on_device
    return jax.shard_map(
        body,
        mesh=mesh,
        in_specs=placed,
        out_specs=(P(("dom", "rep"), None), P(), P()),
        check_vma=False,
    )
```

```python
import functools

import jax
import jax.numpy as jnp
from jax import lax
from jax.experimental import pallas as pl
from jax.experimental.pallas import tpu as pltpu
from jax.sharding import PartitionSpec as P

MESH = pl.DeviceIdType.MESH
UNITS = (3, 2, 1)
CHUNKS = (8, 4, 4)
PARTS = len(UNITS)
F32 = jnp.float32
BF16 = jnp.bfloat16


def spread(value, axis, source):
    kept = jnp.where(lax.axis_index(axis) == source, value, 0).astype(value.dtype)
    return lax.psum(kept, axis)


def section_term(source, tiles, tile_cols, tile_mask, section):
    rblocks = tiles.shape[0]
    tile_side = tiles.shape[3]
    feat_width = source.shape[1]
    source_blocks = source.reshape(source.shape[0] // tile_side, tile_side, feat_width)
    columns = lax.dynamic_index_in_dim(tile_cols, section, 1, keepdims=False)
    live = lax.dynamic_index_in_dim(tile_mask, section, 1, keepdims=False)
    tile_set = lax.dynamic_index_in_dim(tiles, section, 1, keepdims=False)
    block_ids = jnp.arange(source_blocks.shape[0])
    selector = ((columns[:, :, None] == block_ids[None, None, :]) * live[:, :, None]).astype(
        jnp.bfloat16
    )
    picked = jnp.einsum(
        "bkc,cjd->bkjd", selector, source_blocks, preferred_element_type=jnp.float32
    ).astype(jnp.bfloat16)
    summed = jnp.einsum("bkij,bkjd->bid", tile_set, picked, preferred_element_type=jnp.float32)
    return summed.reshape(rblocks * tile_side, feat_width)


def on_device(features, tiles, tile_cols, tile_mask, weight, bias, cotangent):
    sections = tiles.shape[1]
    replica = lax.axis_index("rep")
    aggregate = jnp.zeros(features.shape, jnp.float32)
    for turn_index in range(sections):
        root_index = replica * sections + turn_index
        source = spread(features, "dom", root_index)
        aggregate = aggregate + section_term(source, tiles, tile_cols, tile_mask, turn_index)
    rows_sum = lax.psum_scatter(
        aggregate.astype(jnp.bfloat16), "rep", scatter_dimension=0, tiled=True
    )
    pre_act = jnp.dot(rows_sum, weight, preferred_element_type=jnp.float32) + bias
    sigmoid_pre = jax.nn.sigmoid(pre_act)
    output = (pre_act * sigmoid_pre).astype(jnp.bfloat16)
    grad_pre = cotangent.astype(jnp.float32) * sigmoid_pre * (1.0 + pre_act * (1.0 - sigmoid_pre))
    grad_low = grad_pre.astype(jnp.bfloat16)
    local_weight = jnp.einsum("nd,ne->de", rows_sum, grad_low, preferred_element_type=jnp.float32)
    local_bias = jnp.sum(grad_pre, axis=0)
    grad_weight, grad_bias = lax.psum((local_weight, local_bias), ("dom", "rep"))
    return (output, grad_weight, grad_bias)


ORDERS = (("x", "y", "z"), ("y", "z", "x"), ("z", "x", "y"))
WAYS = {"x": 2, "y": 2, "z": 4}


def part_rows(group_rows, order, stage):
    rows = group_rows
    for axis in order[: stage + 1]:
        rows //= WAYS[axis]
    return rows


def column_parts(width):
    unit = width // sum(UNITS)
    wide = [u * unit for u in UNITS]
    return [(sum(wide[:t]), wide[t]) for t in range(PARTS)]


def kernel(feat_hbm, tiles_hbm, cols_hbm, mask_hbm, weight_hbm, bias_hbm, cot_hbm,
           out_ref, gw_ref, gb_ref,
           slots,
           tiles_v, weight_v, cot_v, cols, mask, bias_ref, dense, acc,
           part_out, part_in, mixed, mixed_t, pre_acc, glow,
           gacc, gsend, gcore_out, gcore_in,
           rb00, rb01, rb02, rb10, rb11, rb12, rb20, rb21, rb22,
           bstate, brecv,
           lsem, zrecv, yrecv, crecv, zup, zdown, ysend, csend,
           psend, precv, gcs, gcr, rs_s, rs_r, ag_s, ag_r, fs, fr, bs, br):
    rbufs = [[rb00, rb01, rb02], [rb10, rb11, rb12], [rb20, rb21, rb22]]
    me = lax.axis_index("dom")
    r = lax.axis_index("rep")
    z = lax.div(me, 4)
    y = lax.rem(lax.div(me, 2), 2)
    c = lax.rem(me, 2)
    w = z + r * (3 - 2 * z)
    dz = 1 - 2 * r
    rblocks, sections, ways, side, _ = tiles_v.shape
    rows, width = feat_hbm.shape
    parts = column_parts(width)
    half = rows // 2

    def dev(zz, yy, cc, rr):
        return (zz * 4 + yy * 2 + cc, rr)

    def z_peer(d):
        z2 = lax.rem(lax.div(z, 2) + d // 2, 2)
        z1 = lax.rem(lax.rem(z, 2) + d % 2, 2)
        return z2 * 2 + z1

    peers = {
        "x": [dev(z, y, c, 1 - r)],
        "y": [dev(z, 1 - y, c, r)],
        "z": [dev(z_peer(d), y, c, r) for d in (1, 2, 3)],
    }
    places = {"x": [1 - r], "y": [1 - y], "z": [z_peer(d) for d in (1, 2, 3)]}
    mine = {"x": r, "y": y, "z": z}
    other_core = dev(z, y, 1 - c, r)
    up = dev(jnp.clip(z + dz, 0, 3), y, c, r)
    down = dev(jnp.clip(z - dz, 0, 3), y, c, r)

    def remote(src, dst, ss, rs, device):
        return pltpu.make_async_remote_copy(
            src_ref=src, dst_ref=dst, send_sem=ss, recv_sem=rs, device_id=device, device_id_type=MESH
        )

    def own_load(i, t):
        return pltpu.make_async_copy(
            feat_hbm.at[:, pl.ds(*parts[t])], slots[i][0][0][t], lsem.at[6 + t]
        )

    for i in range(2):
        @pl.when(w == i)
        def _():
            for t in range(PARTS):
                own_load(i, t).start()
    tiles_load = pltpu.make_async_copy(tiles_hbm, tiles_v, lsem.at[0])
    weight_load = pltpu.make_async_copy(weight_hbm, weight_v, lsem.at[1])
    cot_load = pltpu.make_async_copy(cot_hbm, cot_v, lsem.at[2])
    cols_load = pltpu.make_async_copy(cols_hbm, cols, lsem.at[3])
    mask_load = pltpu.make_async_copy(mask_hbm, mask, lsem.at[4])
    bias_load = pltpu.make_async_copy(bias_hbm, bias_ref, lsem.at[5])
    cols_load.start()
    mask_load.start()
    bias_load.start()
    tiles_load.start()
    weight_load.start()
    cot_load.start()
    barrier = pltpu.get_barrier_semaphore()
    greeted = [other_core] + peers["x"] + peers["y"] + peers["z"]
    for device in greeted:
        pl.semaphore_signal(barrier, inc=1, device_id=device, device_id_type=MESH)
    pl.semaphore_wait(barrier, len(greeted))

    everything = pl.ds(0, rows)

    def chunk(t, ch):
        crows = rows // CHUNKS[t]
        return pl.ds(pl.multiple_of(ch * crows, crows), crows)

    def z_copy(t, i, at, sem, rsem, device):
        slot = slots[i][0][0][t]
        return remote(slot.at[at], slot.at[at], sem, rsem, device)

    def y_copy(t, i, at, rsem):
        return remote(slots[i][0][0][t].at[at], slots[i][1][0][t].at[at],
                      ysend.at[t, i], rsem, peers["y"][0])

    def c_copy(t, i, j, at):
        return remote(slots[i][j][0][t].at[at], slots[i][j][1][t].at[at],
                      csend.at[t, 2 * i + j], crecv.at[t, 2 * i + j], other_core)

    ups = {0: w <= 2, 1: jnp.logical_and(w >= 1, w <= 2)}

    def forward(t, i, ch):
        at = chunk(t, ch)

        @pl.when(ups[i])
        def _():
            z_copy(t, i, at, zup.at[t, i], zrecv.at[t, i, ch], up).start()

        if i == 1:
            @pl.when(w == 1)
            def _():
                z_copy(t, i, at, zdown.at[t], zrecv.at[t, i, ch], down).start()
        y_copy(t, i, at, yrecv.at[t, i, ch]).start()
        c_copy(t, i, 0, at).start()

    def up_sent(t, i):
        z_copy(t, i, everything, zup.at[t, i], zrecv.at[t, i, 0], up).wait_send()

    def own_step(t):
        for i in range(2):
            @pl.when(w == i)
            def _():
                own_load(i, t).wait()
                if t > 0:
                    up_sent(t - 1, i)

                @pl.loop(0, CHUNKS[t])
                def _(ch):
                    forward(t, i, ch)

    def z_step(t, i, ch):
        @pl.when(w != i)
        def _():
            z_copy(t, i, chunk(t, ch), zup.at[t, i], zrecv.at[t, i, ch], up).wait_recv()
            forward(t, i, ch)

    def y_step(t, i, ch):
        y_copy(t, i, chunk(t, ch), yrecv.at[t, i, ch]).wait_recv()
        c_copy(t, i, 1, chunk(t, ch)).start()

    def assemble(index):
        i = 1 - lax.div(index, 4)
        j = lax.rem(lax.div(index, 2), 2)
        k = lax.rem(index, 2)
        zz = i + r * (1 - 2 * i)
        section = zz * 4 + (y + j - 2 * y * j) * 2 + (c + k - 2 * c * k)

        @pl.loop(0, rblocks)
        def _(b):
            tile_of = [tiles_v[b, section, t].astype(F32) for t in range(ways)]
            for block in range(rows // side):
                total = None
                for t in range(ways):
                    take = jnp.logical_and(cols[b, t, section] == block, mask[b, t, section] != 0)
                    term = tile_of[t] * jnp.where(take, 1.0, 0.0)
                    total = term if total is None else total + term
                dense[index, pl.ds(pl.multiple_of(b * side, side), side),
                      block * side:(block + 1) * side] = total.astype(BF16)

    def product(t, i, j, k, at):
        index = (1 - i) * 4 + j * 2 + k
        return jnp.dot(dense[index, at, :], slots[i][j][k][t][...], preferred_element_type=F32)

    def add_product(t, i, j, k):
        if k == 1:
            c_copy(t, i, j, everything).wait_recv()
        term = product(t, i, j, k, everything)
        if (i, j, k) == (1, 0, 0):
            acc[t][...] = term
        else:
            acc[t][...] = acc[t][...] + term

    def p_copy(t):
        return remote(part_out[t], part_in[t], psend.at[t], precv.at[t], peers["x"][0])

    peer_rows = pl.ds(pl.multiple_of((1 - r) * half, half), half)
    own_rows = pl.ds(pl.multiple_of(r * half, half), half)

    def exchange(t):
        part_out[t][...] = acc[t][peer_rows, :].astype(BF16)
        p_copy(t).start()
        mixed[t][...] = acc[t][own_rows, :].astype(BF16)

    def meet(t):
        p_copy(t).wait_recv()
        low = (mixed[t][...].astype(F32) + part_in[t][...].astype(F32)).astype(BF16)
        mixed[t][...] = low
        return jnp.dot(low, weight_v[pl.ds(*parts[t]), :], preferred_element_type=F32)

    jobs = [(j, k) for j in range(2) for k in range(2)]
    order = [(t, i, ch) for t in range(PARTS) for i in (1, 0) for ch in range(CHUNKS[t])]
    lag = 2
    for position, (t, i, ch) in enumerate(order):
        if i == 1 and ch == 0:
            own_step(t)
        if position == 0:
            cols_load.wait()
            mask_load.wait()
            tiles_load.wait()
        z_step(t, i, ch)
        if position >= lag:
            y_step(*order[position - lag])
        each = CHUNKS[t] // 4
        turn = ch // each
        if t == 0 and ch % each == 0:
            assemble((1 - i) * 4 + turn)
        if ch % each == each - 1:
            if i == 0:
                add_product(t, 1, *jobs[turn])
            elif t > 0:
                add_product(t - 1, 0, *jobs[turn])
                if turn == 3:
                    exchange(t - 1)
        if (t, i, ch) == (PARTS - 1, 0, 0):
            weight_load.wait()
            bias_load.wait()
            pre_acc[...] = meet(0) + bias_ref[...].reshape(1, width)
    for behind in range(lag, 0, -1):
        y_step(*order[-behind])
    last = PARTS - 1
    for t in range(1, last):
        pre_acc[...] = pre_acc[...] + meet(t)
    c_copy(last, 0, 0, everything).wait_recv()
    c_copy(last, 0, 1, everything).wait_recv()

    def finish(at, target):
        total = acc[last][at, :]
        for j in range(2):
            for k in range(2):
                total = total + product(last, 0, j, k, at)
        target[last][...] = total.astype(BF16)

    finish(peer_rows, part_out)
    p_copy(last).start()
    finish(own_rows, mixed)
    for t in range(last):
        mixed_t[pl.ds(*parts[t]), :] = mixed[t][...].T
    cot_load.wait()
    pre = pre_acc[...] + meet(last)
    mixed_t[pl.ds(*parts[last]), :] = mixed[last][...].T
    sig = 1.0 / (1.0 + jnp.exp(-pre))
    out_ref[...] = (pre * sig).astype(BF16)
    grad = cot_v[...].astype(F32) * sig * (1.0 + pre * (1.0 - sig))
    glow[...] = grad.astype(BF16)
    bias_rows = jnp.sum(grad.reshape(half // 8, 8, width), axis=0)

    cw = width // 2
    group_rows = width // 3
    own_cols = pl.ds(pl.multiple_of(c * cw, 128), cw)
    other_cols = pl.ds(pl.multiple_of((1 - c) * cw, 128), cw)

    def grad_part(g, start):
        lanes = pl.ds(pl.multiple_of(start, 128), cw)
        return jnp.dot(mixed_t[pl.ds(g * group_rows, group_rows), :], glow[:, lanes], preferred_element_type=F32)

    def b_send(stage, axis_peers, first):
        copies = []
        for d, device in enumerate(axis_peers):
            copies.append(remote(bstate.at[stage], brecv.at[first + d], bs.at[first + d],
                                 br.at[first + d], device))
            copies[-1].start()
        return copies

    def b_sum(stage, copies, first):
        for copy in copies:
            copy.wait_recv()
        total = bstate[stage] + brecv[first]
        if len(copies) == 3:
            total = total + (brecv[first + 1] + brecv[first + 2])
        bstate[stage + 1] = total

    sent = []
    bstate[0] = bias_rows
    core_copies = []
    for g in range(3):
        at = pl.ds(g * group_rows, group_rows)
        gcore_out[at, :] = grad_part(g, (1 - c) * cw).astype(BF16)
        core_copies.append(remote(gcore_out.at[at], gcore_in.at[at], gcs.at[g], gcr.at[g], other_core))
        core_copies[-1].start()
    b_copies = b_send(0, [other_core], 0)
    sent += core_copies + b_copies
    for g in range(3):
        gacc[pl.ds(g * group_rows, group_rows), :] = grad_part(g, c * cw)

    starts = [g * group_rows for g in range(3)]
    history = [[], [], []]
    flying = [None, None, None]

    def scatter(g, stage):
        axis = ORDERS[g][stage]
        size = part_rows(group_rows, ORDERS[g], stage)
        copies = []
        for d, (device, place) in enumerate(zip(peers[axis], places[axis])):
            at = pl.ds(pl.multiple_of(starts[g] + place * size, size), size)
            gsend[at, :] = gacc[at, :].astype(BF16)
            copies.append(remote(gsend.at[at], rbufs[g][stage].at[d],
                                 rs_s.at[g, stage, d], rs_r.at[g, stage, d], device))
            copies[-1].start()
        flying[g] = copies
        sent.extend(copies)

    def gather(g, stage):
        axis = ORDERS[g][stage]
        size = part_rows(group_rows, ORDERS[g], stage)
        at = pl.ds(pl.multiple_of(starts[g], size), size)
        arriving = []
        for d, (device, place) in enumerate(zip(peers[axis], places[axis])):
            copy = remote(gw_ref.at[at, own_cols], gw_ref.at[at, own_cols], ag_s.at[g, stage, d], ag_r.at[g, stage, d], device)
            copy.start()
            sent.append(copy)
            there = pl.ds(pl.multiple_of(history[g][stage] + place * size, size), size)
            arriving.append((there, remote(gw_ref.at[there, own_cols], gw_ref.at[there, own_cols], ag_s.at[g, stage, d],
                                           ag_r.at[g, stage, d], device)))
        starts[g] = history[g][stage]
        flying[g] = arriving

    def to_core(at):
        remote(gw_ref.at[at, own_cols], gw_ref.at[at, own_cols], fs, fr, other_core).start()

    for g in range(3):
        at = pl.ds(g * group_rows, group_rows)
        core_copies[g].wait_recv()
        gacc[at, :] = gacc[at, :] + gcore_in[at, :].astype(F32)
        scatter(g, 0)
    b_sum(0, b_copies, 0)
    b_first = (1, 2, 3)
    for stage in range(3):
        b_copies = b_send(stage + 1, peers[ORDERS[0][stage]], b_first[stage])
        sent += b_copies
        for g, order_g in enumerate(ORDERS):
            size = part_rows(group_rows, order_g, stage)
            for copy in flying[g]:
                copy.wait_recv()
            keep = starts[g] + mine[order_g[stage]] * size
            at = pl.ds(pl.multiple_of(keep, size), size)
            total = gacc[at, :]
            for d in range(len(flying[g])):
                total = total + rbufs[g][stage][d].astype(F32)
            history[g].append(starts[g])
            starts[g] = keep
            if stage < 2:
                gacc[at, :] = total
                scatter(g, stage + 1)
            else:
                gw_ref[at, own_cols] = total.astype(BF16)
                gather(g, 2)
                to_core(at)
        b_sum(stage + 1, b_copies, b_first[stage])
    for stage in (2, 1, 0):
        for g in range(3):
            arriving = flying[g]
            for _, copy in arriving:
                copy.wait_recv()
            if stage > 0:
                gather(g, stage - 1)
            for there, _ in arriving:
                to_core(there)
    gb_ref[...] = jnp.sum(bstate[4], axis=0)
    remote(gw_ref.at[:, other_cols], gw_ref.at[:, other_cols], fs, fr, other_core).wait_recv()
    remote(gw_ref.at[:, own_cols], gw_ref.at[:, own_cols], fs, fr, other_core).wait_send()

    for t in range(PARTS):
        for i in range(2):
            waited = w != i if t < PARTS - 1 else w >= 0

            @pl.when(jnp.logical_and(ups[i], waited))
            def _():
                up_sent(t, i)
            y_copy(t, i, everything, yrecv.at[t, i, 0]).wait_send()
            for j in range(2):
                c_copy(t, i, j, everything).wait_send()

        @pl.when(w == 1)
        def _():
            z_copy(t, 1, everything, zdown.at[t], zrecv.at[t, 1, 0], down).wait_send()
        p_copy(t).wait_send()
    for copy in sent:
        copy.wait_send()


def in_kernel(features, tiles, tile_cols, tile_mask, weight, bias, cotangent):
    rows, width = features.shape
    half = rows // 2
    cw = width // 2
    parts = column_parts(width)
    vmem = pl.BlockSpec(memory_space=pltpu.VMEM)
    hbm = pl.BlockSpec(memory_space=pltpu.HBM)
    dma = pltpu.SemaphoreType.DMA
    most = max(CHUNKS)

    def columns(height, dtype):
        return [pltpu.VMEM((height, wide), dtype) for _, wide in parts]

    rbufs = [
        pltpu.VMEM((WAYS[order[stage]] - 1, part_rows(width // 3, order, stage), cw), BF16)
        for order in ORDERS
        for stage in range(3)
    ]
    out, grad_weight, grad_bias = pl.pallas_call(
        kernel,
        out_shape=(
            jax.ShapeDtypeStruct((half, width), BF16),
            jax.ShapeDtypeStruct((width, width), BF16),
            jax.ShapeDtypeStruct((width,), F32),
        ),
        in_specs=[hbm] * 7,
        out_specs=(vmem, vmem, vmem),
        scratch_shapes=[
            [[[columns(rows, BF16)] * 2] * 2] * 2,
            pltpu.VMEM(tiles.shape, BF16),
            pltpu.VMEM(weight.shape, BF16),
            pltpu.VMEM(cotangent.shape, BF16),
            pltpu.SMEM((tiles.shape[0], tiles.shape[2], tiles.shape[1]), jnp.int32),
            pltpu.SMEM((tiles.shape[0], tiles.shape[2], tiles.shape[1]), jnp.int32),
            pltpu.VMEM((width,), F32),
            pltpu.VMEM((8, rows, rows), BF16),
            columns(rows, F32),
            columns(half, BF16),
            columns(half, BF16),
            columns(half, BF16),
            pltpu.VMEM((width, half), BF16),
            pltpu.VMEM((half, width), F32),
            pltpu.VMEM((half, width), BF16),
            pltpu.VMEM((width, cw), F32),
        ]
        + [pltpu.VMEM((width, cw), BF16)] * 3
        + rbufs
        + [
            pltpu.VMEM((5, 8, width), F32),
            pltpu.VMEM((6, 8, width), F32),
            dma((6 + PARTS,)), dma((PARTS, 2, most)), dma((PARTS, 2, most)), dma((PARTS, 4)),
            dma((PARTS, 2)), dma((PARTS,)), dma((PARTS, 2)), dma((PARTS, 4)),
            dma((PARTS,)), dma((PARTS,)), dma((3,)), dma((3,)),
            dma((3, 3, 3)), dma((3, 3, 3)), dma((3, 3, 3)), dma((3, 3, 3)),
            dma, dma, dma((6,)), dma((6,)),
        ],
        compiler_params=pltpu.CompilerParams(
            collective_id=0, has_side_effects=True, vmem_limit_bytes=63 * 1024 * 1024
        ),
    )(features, tiles, tile_cols.transpose(0, 2, 1), tile_mask.transpose(0, 2, 1), weight, bias, cotangent)
    return out, grad_weight.astype(F32), grad_bias


def solution(mesh):
    placed = (
        P("dom", None),
        P("dom", "rep", None, None, None),
        P("dom", "rep", None),
        P("dom", "rep", None),
        P(),
        P(),
        P(("dom", "rep"), None),
    )
    body = in_kernel if (mesh.shape["dom"], mesh.shape["rep"]) == (16, 2) else on_device
    return jax.shard_map(
        body,
        mesh=mesh,
        in_specs=placed,
        out_specs=(P(("dom", "rep"), None), P(), P()),
        check_vma=False,
    )
```

```python
import functools

import jax
import jax.numpy as jnp
from jax import lax
from jax.experimental import pallas as pl
from jax.experimental.pallas import tpu as pltpu
from jax.sharding import PartitionSpec as P

MESH = pl.DeviceIdType.MESH
UNITS = (2, 2, 2)
CHUNKS = (4, 4, 4)
PARTS = len(UNITS)
F32 = jnp.float32
BF16 = jnp.bfloat16


def spread(value, axis, source):
    kept = jnp.where(lax.axis_index(axis) == source, value, 0).astype(value.dtype)
    return lax.psum(kept, axis)


def section_term(source, tiles, tile_cols, tile_mask, section):
    rblocks = tiles.shape[0]
    tile_side = tiles.shape[3]
    feat_width = source.shape[1]
    source_blocks = source.reshape(source.shape[0] // tile_side, tile_side, feat_width)
    columns = lax.dynamic_index_in_dim(tile_cols, section, 1, keepdims=False)
    live = lax.dynamic_index_in_dim(tile_mask, section, 1, keepdims=False)
    tile_set = lax.dynamic_index_in_dim(tiles, section, 1, keepdims=False)
    block_ids = jnp.arange(source_blocks.shape[0])
    selector = ((columns[:, :, None] == block_ids[None, None, :]) * live[:, :, None]).astype(
        jnp.bfloat16
    )
    picked = jnp.einsum(
        "bkc,cjd->bkjd", selector, source_blocks, preferred_element_type=jnp.float32
    ).astype(jnp.bfloat16)
    summed = jnp.einsum("bkij,bkjd->bid", tile_set, picked, preferred_element_type=jnp.float32)
    return summed.reshape(rblocks * tile_side, feat_width)


def on_device(features, tiles, tile_cols, tile_mask, weight, bias, cotangent):
    sections = tiles.shape[1]
    replica = lax.axis_index("rep")
    aggregate = jnp.zeros(features.shape, jnp.float32)
    for turn_index in range(sections):
        root_index = replica * sections + turn_index
        source = spread(features, "dom", root_index)
        aggregate = aggregate + section_term(source, tiles, tile_cols, tile_mask, turn_index)
    rows_sum = lax.psum_scatter(
        aggregate.astype(jnp.bfloat16), "rep", scatter_dimension=0, tiled=True
    )
    pre_act = jnp.dot(rows_sum, weight, preferred_element_type=jnp.float32) + bias
    sigmoid_pre = jax.nn.sigmoid(pre_act)
    output = (pre_act * sigmoid_pre).astype(jnp.bfloat16)
    grad_pre = cotangent.astype(jnp.float32) * sigmoid_pre * (1.0 + pre_act * (1.0 - sigmoid_pre))
    grad_low = grad_pre.astype(jnp.bfloat16)
    local_weight = jnp.einsum("nd,ne->de", rows_sum, grad_low, preferred_element_type=jnp.float32)
    local_bias = jnp.sum(grad_pre, axis=0)
    grad_weight, grad_bias = lax.psum((local_weight, local_bias), ("dom", "rep"))
    return (output, grad_weight, grad_bias)


ORDERS = (("x", "y", "z"), ("y", "z", "x"), ("z", "x", "y"))
WAYS = {"x": 2, "y": 2, "z": 4}


def part_rows(group_rows, order, stage):
    rows = group_rows
    for axis in order[: stage + 1]:
        rows //= WAYS[axis]
    return rows


def column_parts(width):
    unit = width // sum(UNITS)
    wide = [u * unit for u in UNITS]
    return [(sum(wide[:t]), wide[t]) for t in range(PARTS)]


def kernel(feat_hbm, tiles_hbm, cols_hbm, mask_hbm, weight_hbm, bias_hbm, cot_hbm,
           out_ref, gw_ref, gb_ref,
           slots,
           tiles_v, weight_v, cot_v, cols, mask, bias_ref, dense, acc,
           part_out, part_in, mixed, mixed_t, pre_acc, glow,
           gacc, gsend, gcore_out, gcore_in,
           rb00, rb01, rb02, rb10, rb11, rb12, rb20, rb21, rb22,
           bstate, brecv,
           lsem, zrecv, yrecv, crecv, zup, zdown, ysend, csend,
           psend, precv, gcs, gcr, rs_s, rs_r, ag_s, ag_r, fs, fr, bs, br):
    rbufs = [[rb00, rb01, rb02], [rb10, rb11, rb12], [rb20, rb21, rb22]]
    me = lax.axis_index("dom")
    r = lax.axis_index("rep")
    z = lax.div(me, 4)
    y = lax.rem(lax.div(me, 2), 2)
    c = lax.rem(me, 2)
    w = z + r * (3 - 2 * z)
    dz = 1 - 2 * r
    rblocks, sections, ways, side, _ = tiles_v.shape
    rows, width = feat_hbm.shape
    parts = column_parts(width)
    half = rows // 2

    def dev(zz, yy, cc, rr):
        return (zz * 4 + yy * 2 + cc, rr)

    def z_peer(d):
        z2 = lax.rem(lax.div(z, 2) + d // 2, 2)
        z1 = lax.rem(lax.rem(z, 2) + d % 2, 2)
        return z2 * 2 + z1

    peers = {
        "x": [dev(z, y, c, 1 - r)],
        "y": [dev(z, 1 - y, c, r)],
        "z": [dev(z_peer(d), y, c, r) for d in (1, 2, 3)],
    }
    places = {"x": [1 - r], "y": [1 - y], "z": [z_peer(d) for d in (1, 2, 3)]}
    mine = {"x": r, "y": y, "z": z}
    other_core = dev(z, y, 1 - c, r)
    up = dev(jnp.clip(z + dz, 0, 3), y, c, r)
    down = dev(jnp.clip(z - dz, 0, 3), y, c, r)

    def remote(src, dst, ss, rs, device):
        return pltpu.make_async_remote_copy(
            src_ref=src, dst_ref=dst, send_sem=ss, recv_sem=rs, device_id=device, device_id_type=MESH
        )

    def own_load(i, t):
        return pltpu.make_async_copy(
            feat_hbm.at[:, pl.ds(*parts[t])], slots[i][0][0][t], lsem.at[6 + t]
        )

    for i in range(2):
        @pl.when(w == i)
        def _():
            for t in range(PARTS):
                own_load(i, t).start()
    tiles_load = pltpu.make_async_copy(tiles_hbm, tiles_v, lsem.at[0])
    weight_load = pltpu.make_async_copy(weight_hbm, weight_v, lsem.at[1])
    cot_load = pltpu.make_async_copy(cot_hbm, cot_v, lsem.at[2])
    cols_load = pltpu.make_async_copy(cols_hbm, cols, lsem.at[3])
    mask_load = pltpu.make_async_copy(mask_hbm, mask, lsem.at[4])
    bias_load = pltpu.make_async_copy(bias_hbm, bias_ref, lsem.at[5])
    cols_load.start()
    mask_load.start()
    bias_load.start()
    tiles_load.start()
    weight_load.start()
    cot_load.start()
    barrier = pltpu.get_barrier_semaphore()
    greeted = [other_core] + peers["x"] + peers["y"] + peers["z"]
    for device in greeted:
        pl.semaphore_signal(barrier, inc=1, device_id=device, device_id_type=MESH)
    pl.semaphore_wait(barrier, len(greeted))

    everything = pl.ds(0, rows)

    def chunk(t, ch):
        crows = rows // CHUNKS[t]
        return pl.ds(pl.multiple_of(ch * crows, crows), crows)

    def z_copy(t, i, at, sem, rsem, device):
        slot = slots[i][0][0][t]
        return remote(slot.at[at], slot.at[at], sem, rsem, device)

    def y_copy(t, i, at, rsem):
        return remote(slots[i][0][0][t].at[at], slots[i][1][0][t].at[at],
                      ysend.at[t, i], rsem, peers["y"][0])

    def c_copy(t, i, j, at):
        return remote(slots[i][j][0][t].at[at], slots[i][j][1][t].at[at],
                      csend.at[t, 2 * i + j], crecv.at[t, 2 * i + j], other_core)

    ups = {0: w <= 2, 1: jnp.logical_and(w >= 1, w <= 2)}

    def forward(t, i, ch):
        at = chunk(t, ch)

        @pl.when(ups[i])
        def _():
            z_copy(t, i, at, zup.at[t, i], zrecv.at[t, i, ch], up).start()

        if i == 1:
            @pl.when(w == 1)
            def _():
                z_copy(t, i, at, zdown.at[t], zrecv.at[t, i, ch], down).start()
        y_copy(t, i, at, yrecv.at[t, i, ch]).start()

    def up_sent(t, i):
        z_copy(t, i, everything, zup.at[t, i], zrecv.at[t, i, 0], up).wait_send()

    def own_step(t):
        for i in range(2):
            @pl.when(w == i)
            def _():
                own_load(i, t).wait()
                if t > 0:
                    up_sent(t - 1, i)

                @pl.loop(0, CHUNKS[t])
                def _(ch):
                    forward(t, i, ch)
                c_copy(t, i, 0, everything).start()

    def z_step(t, i, ch):
        @pl.when(w != i)
        def _():
            z_copy(t, i, chunk(t, ch), zup.at[t, i], zrecv.at[t, i, ch], up).wait_recv()
            forward(t, i, ch)
            if ch == CHUNKS[t] - 1:
                c_copy(t, i, 0, everything).start()

    def y_step(t, i, ch):
        y_copy(t, i, chunk(t, ch), yrecv.at[t, i, ch]).wait_recv()
        if ch == CHUNKS[t] - 1:
            c_copy(t, i, 1, everything).start()

    def assemble(index):
        i = 1 - lax.div(index, 4)
        j = lax.rem(lax.div(index, 2), 2)
        k = lax.rem(index, 2)
        zz = i + r * (1 - 2 * i)
        section = zz * 4 + (y + j - 2 * y * j) * 2 + (c + k - 2 * c * k)

        @pl.loop(0, rblocks)
        def _(b):
            tile_of = [tiles_v[b, section, t].astype(F32) for t in range(ways)]
            for block in range(rows // side):
                total = None
                for t in range(ways):
                    take = jnp.logical_and(cols[b, t, section] == block, mask[b, t, section] != 0)
                    term = tile_of[t] * jnp.where(take, 1.0, 0.0)
                    total = term if total is None else total + term
                dense[index, pl.ds(pl.multiple_of(b * side, side), side),
                      block * side:(block + 1) * side] = total.astype(BF16)

    def product(t, i, j, k, at):
        index = (1 - i) * 4 + j * 2 + k
        return jnp.dot(dense[index, at, :], slots[i][j][k][t][...], preferred_element_type=F32)

    def add_product(t, i, j, k):
        if k == 1:
            c_copy(t, i, j, everything).wait_recv()
        term = product(t, i, j, k, everything)
        if (i, j, k) == (1, 0, 0):
            acc[t][...] = term
        else:
            acc[t][...] = acc[t][...] + term

    def p_copy(t):
        return remote(part_out[t], part_in[t], psend.at[t], precv.at[t], peers["x"][0])

    peer_rows = pl.ds(pl.multiple_of((1 - r) * half, half), half)
    own_rows = pl.ds(pl.multiple_of(r * half, half), half)

    def exchange(t):
        part_out[t][...] = acc[t][peer_rows, :].astype(BF16)
        p_copy(t).start()
        mixed[t][...] = acc[t][own_rows, :].astype(BF16)

    def meet(t):
        p_copy(t).wait_recv()
        low = (mixed[t][...].astype(F32) + part_in[t][...].astype(F32)).astype(BF16)
        mixed[t][...] = low
        return jnp.dot(low, weight_v[pl.ds(*parts[t]), :], preferred_element_type=F32)

    jobs = [(j, k) for j in range(2) for k in range(2)]
    order = [(t, i, ch) for t in range(PARTS) for i in (1, 0) for ch in range(CHUNKS[t])]
    lag = 2
    for position, (t, i, ch) in enumerate(order):
        if i == 1 and ch == 0:
            own_step(t)
        if position == 0:
            cols_load.wait()
            mask_load.wait()
            tiles_load.wait()
        z_step(t, i, ch)
        if position >= lag:
            y_step(*order[position - lag])
        each = CHUNKS[t] // 4
        turn = ch // each
        if t == 0 and ch % each == 0:
            assemble((1 - i) * 4 + turn)
        if ch % each == each - 1:
            if i == 0:
                add_product(t, 1, *jobs[turn])
            elif t > 0:
                add_product(t - 1, 0, *jobs[turn])
                if turn == 3:
                    exchange(t - 1)
        if (t, i, ch) == (PARTS - 1, 0, 0):
            weight_load.wait()
            bias_load.wait()
            pre_acc[...] = meet(0) + bias_ref[...].reshape(1, width)
    for behind in range(lag, 0, -1):
        y_step(*order[-behind])
    last = PARTS - 1
    for t in range(1, last):
        pre_acc[...] = pre_acc[...] + meet(t)
    c_copy(last, 0, 0, everything).wait_recv()
    c_copy(last, 0, 1, everything).wait_recv()

    def finish(at, target):
        total = acc[last][at, :]
        for j in range(2):
            for k in range(2):
                total = total + product(last, 0, j, k, at)
        target[last][...] = total.astype(BF16)

    finish(peer_rows, part_out)
    p_copy(last).start()
    finish(own_rows, mixed)
    for t in range(last):
        mixed_t[pl.ds(*parts[t]), :] = mixed[t][...].T
    cot_load.wait()
    pre = pre_acc[...] + meet(last)
    mixed_t[pl.ds(*parts[last]), :] = mixed[last][...].T
    sig = 1.0 / (1.0 + jnp.exp(-pre))
    out_ref[...] = (pre * sig).astype(BF16)
    grad = cot_v[...].astype(F32) * sig * (1.0 + pre * (1.0 - sig))
    glow[...] = grad.astype(BF16)
    bias_rows = jnp.sum(grad.reshape(half // 8, 8, width), axis=0)

    cw = width // 2
    group_rows = width // 3
    own_cols = pl.ds(pl.multiple_of(c * cw, 128), cw)
    other_cols = pl.ds(pl.multiple_of((1 - c) * cw, 128), cw)

    def grad_part(g, start):
        lanes = pl.ds(pl.multiple_of(start, 128), cw)
        return jnp.dot(mixed_t[pl.ds(g * group_rows, group_rows), :], glow[:, lanes], preferred_element_type=F32)

    def b_send(stage, axis_peers, first):
        copies = []
        for d, device in enumerate(axis_peers):
            copies.append(remote(bstate.at[stage], brecv.at[first + d], bs.at[first + d],
                                 br.at[first + d], device))
            copies[-1].start()
        return copies

    def b_sum(stage, copies, first):
        for copy in copies:
            copy.wait_recv()
        total = bstate[stage] + brecv[first]
        if len(copies) == 3:
            total = total + (brecv[first + 1] + brecv[first + 2])
        bstate[stage + 1] = total

    sent = []
    bstate[0] = bias_rows
    core_copies = []
    for g in range(3):
        at = pl.ds(g * group_rows, group_rows)
        gcore_out[at, :] = grad_part(g, (1 - c) * cw).astype(BF16)
        core_copies.append(remote(gcore_out.at[at], gcore_in.at[at], gcs.at[g], gcr.at[g], other_core))
        core_copies[-1].start()
    b_copies = b_send(0, [other_core], 0)
    sent += core_copies + b_copies
    for g in range(3):
        gacc[pl.ds(g * group_rows, group_rows), :] = grad_part(g, c * cw)

    starts = [g * group_rows for g in range(3)]
    history = [[], [], []]
    flying = [None, None, None]

    def scatter(g, stage):
        axis = ORDERS[g][stage]
        size = part_rows(group_rows, ORDERS[g], stage)
        copies = []
        for d, (device, place) in enumerate(zip(peers[axis], places[axis])):
            at = pl.ds(pl.multiple_of(starts[g] + place * size, size), size)
            gsend[at, :] = gacc[at, :].astype(BF16)
            copies.append(remote(gsend.at[at], rbufs[g][stage].at[d],
                                 rs_s.at[g, stage, d], rs_r.at[g, stage, d], device))
            copies[-1].start()
        flying[g] = copies
        sent.extend(copies)

    def gather(g, stage):
        axis = ORDERS[g][stage]
        size = part_rows(group_rows, ORDERS[g], stage)
        at = pl.ds(pl.multiple_of(starts[g], size), size)
        arriving = []
        for d, (device, place) in enumerate(zip(peers[axis], places[axis])):
            copy = remote(gw_ref.at[at, own_cols], gw_ref.at[at, own_cols], ag_s.at[g, stage, d], ag_r.at[g, stage, d], device)
            copy.start()
            sent.append(copy)
            there = pl.ds(pl.multiple_of(history[g][stage] + place * size, size), size)
            arriving.append((there, remote(gw_ref.at[there, own_cols], gw_ref.at[there, own_cols], ag_s.at[g, stage, d],
                                           ag_r.at[g, stage, d], device)))
        starts[g] = history[g][stage]
        flying[g] = arriving

    def to_core(at):
        remote(gw_ref.at[at, own_cols], gw_ref.at[at, own_cols], fs, fr, other_core).start()

    for g in range(3):
        at = pl.ds(g * group_rows, group_rows)
        core_copies[g].wait_recv()
        gacc[at, :] = gacc[at, :] + gcore_in[at, :].astype(F32)
        scatter(g, 0)
    b_sum(0, b_copies, 0)
    b_first = (1, 2, 3)
    for stage in range(3):
        b_copies = b_send(stage + 1, peers[ORDERS[0][stage]], b_first[stage])
        sent += b_copies
        for g, order_g in enumerate(ORDERS):
            size = part_rows(group_rows, order_g, stage)
            for copy in flying[g]:
                copy.wait_recv()
            keep = starts[g] + mine[order_g[stage]] * size
            at = pl.ds(pl.multiple_of(keep, size), size)
            total = gacc[at, :]
            for d in range(len(flying[g])):
                total = total + rbufs[g][stage][d].astype(F32)
            history[g].append(starts[g])
            starts[g] = keep
            if stage < 2:
                gacc[at, :] = total
                scatter(g, stage + 1)
            else:
                gw_ref[at, own_cols] = total.astype(BF16)
                gather(g, 2)
                to_core(at)
        b_sum(stage + 1, b_copies, b_first[stage])
    for stage in (2, 1, 0):
        for g in range(3):
            arriving = flying[g]
            for _, copy in arriving:
                copy.wait_recv()
            if stage > 0:
                gather(g, stage - 1)
            for there, _ in arriving:
                to_core(there)
    gb_ref[...] = jnp.sum(bstate[4], axis=0)
    remote(gw_ref.at[:, other_cols], gw_ref.at[:, other_cols], fs, fr, other_core).wait_recv()
    remote(gw_ref.at[:, own_cols], gw_ref.at[:, own_cols], fs, fr, other_core).wait_send()

    for t in range(PARTS):
        for i in range(2):
            waited = w != i if t < PARTS - 1 else w >= 0

            @pl.when(jnp.logical_and(ups[i], waited))
            def _():
                up_sent(t, i)
            y_copy(t, i, everything, yrecv.at[t, i, 0]).wait_send()
            for j in range(2):
                c_copy(t, i, j, everything).wait_send()

        @pl.when(w == 1)
        def _():
            z_copy(t, 1, everything, zdown.at[t], zrecv.at[t, 1, 0], down).wait_send()
        p_copy(t).wait_send()
    for copy in sent:
        copy.wait_send()


def in_kernel(features, tiles, tile_cols, tile_mask, weight, bias, cotangent):
    rows, width = features.shape
    half = rows // 2
    cw = width // 2
    parts = column_parts(width)
    vmem = pl.BlockSpec(memory_space=pltpu.VMEM)
    hbm = pl.BlockSpec(memory_space=pltpu.HBM)
    dma = pltpu.SemaphoreType.DMA
    most = max(CHUNKS)

    def columns(height, dtype):
        return [pltpu.VMEM((height, wide), dtype) for _, wide in parts]

    rbufs = [
        pltpu.VMEM((WAYS[order[stage]] - 1, part_rows(width // 3, order, stage), cw), BF16)
        for order in ORDERS
        for stage in range(3)
    ]
    out, grad_weight, grad_bias = pl.pallas_call(
        kernel,
        out_shape=(
            jax.ShapeDtypeStruct((half, width), BF16),
            jax.ShapeDtypeStruct((width, width), BF16),
            jax.ShapeDtypeStruct((width,), F32),
        ),
        in_specs=[hbm] * 7,
        out_specs=(vmem, vmem, vmem),
        scratch_shapes=[
            [[[columns(rows, BF16)] * 2] * 2] * 2,
            pltpu.VMEM(tiles.shape, BF16),
            pltpu.VMEM(weight.shape, BF16),
            pltpu.VMEM(cotangent.shape, BF16),
            pltpu.SMEM((tiles.shape[0], tiles.shape[2], tiles.shape[1]), jnp.int32),
            pltpu.SMEM((tiles.shape[0], tiles.shape[2], tiles.shape[1]), jnp.int32),
            pltpu.VMEM((width,), F32),
            pltpu.VMEM((8, rows, rows), BF16),
            columns(rows, F32),
            columns(half, BF16),
            columns(half, BF16),
            columns(half, BF16),
            pltpu.VMEM((width, half), BF16),
            pltpu.VMEM((half, width), F32),
            pltpu.VMEM((half, width), BF16),
            pltpu.VMEM((width, cw), F32),
        ]
        + [pltpu.VMEM((width, cw), BF16)] * 3
        + rbufs
        + [
            pltpu.VMEM((5, 8, width), F32),
            pltpu.VMEM((6, 8, width), F32),
            dma((6 + PARTS,)), dma((PARTS, 2, most)), dma((PARTS, 2, most)), dma((PARTS, 4)),
            dma((PARTS, 2)), dma((PARTS,)), dma((PARTS, 2)), dma((PARTS, 4)),
            dma((PARTS,)), dma((PARTS,)), dma((3,)), dma((3,)),
            dma((3, 3, 3)), dma((3, 3, 3)), dma((3, 3, 3)), dma((3, 3, 3)),
            dma, dma, dma((6,)), dma((6,)),
        ],
        compiler_params=pltpu.CompilerParams(
            collective_id=0, has_side_effects=True, vmem_limit_bytes=63 * 1024 * 1024
        ),
    )(features, tiles, tile_cols.transpose(0, 2, 1), tile_mask.transpose(0, 2, 1), weight, bias, cotangent)
    return out, grad_weight.astype(F32), grad_bias


def solution(mesh):
    placed = (
        P("dom", None),
        P("dom", "rep", None, None, None),
        P("dom", "rep", None),
        P("dom", "rep", None),
        P(),
        P(),
        P(("dom", "rep"), None),
    )
    body = in_kernel if (mesh.shape["dom"], mesh.shape["rep"]) == (16, 2) else on_device
    return jax.shard_map(
        body,
        mesh=mesh,
        in_specs=placed,
        out_specs=(P(("dom", "rep"), None), P(), P()),
        check_vma=False,
    )
```

```python
import functools

import jax
import jax.numpy as jnp
from jax import lax
from jax.experimental import pallas as pl
from jax.experimental.pallas import tpu as pltpu
from jax.sharding import PartitionSpec as P

MESH = pl.DeviceIdType.MESH
CHUNKS = 4
THIRDS = 3
F32 = jnp.float32
BF16 = jnp.bfloat16


def spread(value, axis, source):
    kept = jnp.where(lax.axis_index(axis) == source, value, 0).astype(value.dtype)
    return lax.psum(kept, axis)


def section_term(source, tiles, tile_cols, tile_mask, section):
    rblocks = tiles.shape[0]
    tile_side = tiles.shape[3]
    feat_width = source.shape[1]
    source_blocks = source.reshape(source.shape[0] // tile_side, tile_side, feat_width)
    columns = lax.dynamic_index_in_dim(tile_cols, section, 1, keepdims=False)
    live = lax.dynamic_index_in_dim(tile_mask, section, 1, keepdims=False)
    tile_set = lax.dynamic_index_in_dim(tiles, section, 1, keepdims=False)
    block_ids = jnp.arange(source_blocks.shape[0])
    selector = ((columns[:, :, None] == block_ids[None, None, :]) * live[:, :, None]).astype(
        jnp.bfloat16
    )
    picked = jnp.einsum(
        "bkc,cjd->bkjd", selector, source_blocks, preferred_element_type=jnp.float32
    ).astype(jnp.bfloat16)
    summed = jnp.einsum("bkij,bkjd->bid", tile_set, picked, preferred_element_type=jnp.float32)
    return summed.reshape(rblocks * tile_side, feat_width)


def on_device(features, tiles, tile_cols, tile_mask, weight, bias, cotangent):
    sections = tiles.shape[1]
    replica = lax.axis_index("rep")
    aggregate = jnp.zeros(features.shape, jnp.float32)
    for turn_index in range(sections):
        root_index = replica * sections + turn_index
        source = spread(features, "dom", root_index)
        aggregate = aggregate + section_term(source, tiles, tile_cols, tile_mask, turn_index)
    rows_sum = lax.psum_scatter(
        aggregate.astype(jnp.bfloat16), "rep", scatter_dimension=0, tiled=True
    )
    pre_act = jnp.dot(rows_sum, weight, preferred_element_type=jnp.float32) + bias
    sigmoid_pre = jax.nn.sigmoid(pre_act)
    output = (pre_act * sigmoid_pre).astype(jnp.bfloat16)
    grad_pre = cotangent.astype(jnp.float32) * sigmoid_pre * (1.0 + pre_act * (1.0 - sigmoid_pre))
    grad_low = grad_pre.astype(jnp.bfloat16)
    local_weight = jnp.einsum("nd,ne->de", rows_sum, grad_low, preferred_element_type=jnp.float32)
    local_bias = jnp.sum(grad_pre, axis=0)
    grad_weight, grad_bias = lax.psum((local_weight, local_bias), ("dom", "rep"))
    return (output, grad_weight, grad_bias)


ORDERS = (("x", "y", "z"), ("y", "z", "x"), ("z", "x", "y"))
WAYS = {"x": 2, "y": 2, "z": 4}


def part_rows(group_rows, order, stage):
    rows = group_rows
    for axis in order[: stage + 1]:
        rows //= WAYS[axis]
    return rows


def kernel(feat_hbm, tiles_hbm, cols_hbm, mask_hbm, weight_hbm, bias_hbm, cot_hbm,
           out_ref, gw_ref, gb_ref,
           s000, s001, s010, s011, s100, s101, s110, s111,
           tiles_v, weight_v, cot_v, cols, mask, bias_ref, dense, acc,
           part_out, part_in, mixed, mixed_t, pre_acc, glow,
           gacc, gsend, gcore_out, gcore_in,
           rb00, rb01, rb02, rb10, rb11, rb12, rb20, rb21, rb22,
           bstate, brecv,
           lsem, zrecv, yrecv, crecv, zup, zdown, ysend, csend,
           psend, precv, gcs, gcr, rs_s, rs_r, ag_s, ag_r, fs, fr, bs, br):
    slots = [[[s000, s001], [s010, s011]], [[s100, s101], [s110, s111]]]
    rbufs = [[rb00, rb01, rb02], [rb10, rb11, rb12], [rb20, rb21, rb22]]
    me = lax.axis_index("dom")
    r = lax.axis_index("rep")
    z = lax.div(me, 4)
    y = lax.rem(lax.div(me, 2), 2)
    c = lax.rem(me, 2)
    w = z + r * (3 - 2 * z)
    dz = 1 - 2 * r
    rblocks, sections, ways, side, _ = tiles_v.shape
    _, rows, tw = acc.shape
    width = THIRDS * tw
    crows = rows // CHUNKS
    half = rows // 2

    def dev(zz, yy, cc, rr):
        return (zz * 4 + yy * 2 + cc, rr)

    def z_peer(d):
        z2 = lax.rem(lax.div(z, 2) + d // 2, 2)
        z1 = lax.rem(lax.rem(z, 2) + d % 2, 2)
        return z2 * 2 + z1

    peers = {
        "x": [dev(z, y, c, 1 - r)],
        "y": [dev(z, 1 - y, c, r)],
        "z": [dev(z_peer(d), y, c, r) for d in (1, 2, 3)],
    }
    places = {"x": [1 - r], "y": [1 - y], "z": [z_peer(d) for d in (1, 2, 3)]}
    mine = {"x": r, "y": y, "z": z}
    other_core = dev(z, y, 1 - c, r)
    up = dev(jnp.clip(z + dz, 0, 3), y, c, r)
    down = dev(jnp.clip(z - dz, 0, 3), y, c, r)

    def remote(src, dst, ss, rs, device):
        return pltpu.make_async_remote_copy(
            src_ref=src, dst_ref=dst, send_sem=ss, recv_sem=rs, device_id=device, device_id_type=MESH
        )

    def own_load(i, t):
        return pltpu.make_async_copy(
            feat_hbm.at[:, t * tw:(t + 1) * tw], slots[i][0][0].at[t], lsem.at[6 + t]
        )

    for i in range(2):
        @pl.when(w == i)
        def _():
            for t in range(THIRDS):
                own_load(i, t).start()
    tiles_load = pltpu.make_async_copy(tiles_hbm, tiles_v, lsem.at[0])
    weight_load = pltpu.make_async_copy(weight_hbm, weight_v, lsem.at[1])
    cot_load = pltpu.make_async_copy(cot_hbm, cot_v, lsem.at[2])
    cols_load = pltpu.make_async_copy(cols_hbm, cols, lsem.at[3])
    mask_load = pltpu.make_async_copy(mask_hbm, mask, lsem.at[4])
    bias_load = pltpu.make_async_copy(bias_hbm, bias_ref, lsem.at[5])
    cols_load.start()
    mask_load.start()
    bias_load.start()
    tiles_load.start()
    weight_load.start()
    cot_load.start()
    barrier = pltpu.get_barrier_semaphore()
    greeted = [other_core] + peers["x"] + peers["y"] + peers["z"]
    for device in greeted:
        pl.semaphore_signal(barrier, inc=1, device_id=device, device_id_type=MESH)
    pl.semaphore_wait(barrier, len(greeted))

    everything = pl.ds(0, rows)

    def chunk(ch):
        return pl.ds(pl.multiple_of(ch * crows, crows), crows)

    def z_copy(t, i, at, sem, rsem, device):
        slot = slots[i][0][0]
        return remote(slot.at[t, at], slot.at[t, at], sem, rsem, device)

    def y_copy(t, i, at, rsem):
        return remote(slots[i][0][0].at[t, at], slots[i][1][0].at[t, at],
                      ysend.at[t, i], rsem, peers["y"][0])

    def c_copy(t, i, j, at):
        return remote(slots[i][j][0].at[t, at], slots[i][j][1].at[t, at],
                      csend.at[t, 2 * i + j], crecv.at[t, 2 * i + j], other_core)

    ups = {0: w <= 2, 1: jnp.logical_and(w >= 1, w <= 2)}

    def forward(t, i, ch):
        at = chunk(ch)

        @pl.when(ups[i])
        def _():
            z_copy(t, i, at, zup.at[t, i], zrecv.at[t, i, ch], up).start()

        if i == 1:
            @pl.when(w == 1)
            def _():
                z_copy(t, i, at, zdown.at[t], zrecv.at[t, i, ch], down).start()
        y_copy(t, i, at, yrecv.at[t, i, ch]).start()
        c_copy(t, i, 0, at).start()

    def up_sent(t, i):
        z_copy(t, i, everything, zup.at[t, i], zrecv.at[t, i, 0], up).wait_send()

    def own_step(t):
        for i in range(2):
            @pl.when(w == i)
            def _():
                own_load(i, t).wait()
                if t > 0:
                    up_sent(t - 1, i)

                @pl.loop(0, CHUNKS)
                def _(ch):
                    forward(t, i, ch)

    def z_step(t, i, ch):
        @pl.when(w != i)
        def _():
            z_copy(t, i, chunk(ch), zup.at[t, i], zrecv.at[t, i, ch], up).wait_recv()
            forward(t, i, ch)

    def y_step(t, i, ch):
        y_copy(t, i, chunk(ch), yrecv.at[t, i, ch]).wait_recv()
        c_copy(t, i, 1, chunk(ch)).start()

    def assemble(index):
        i = 1 - lax.div(index, 4)
        j = lax.rem(lax.div(index, 2), 2)
        k = lax.rem(index, 2)
        zz = i + r * (1 - 2 * i)
        section = zz * 4 + (y + j - 2 * y * j) * 2 + (c + k - 2 * c * k)

        @pl.loop(0, rblocks)
        def _(b):
            tile_of = [tiles_v[b, section, t].astype(F32) for t in range(ways)]
            for block in range(rows // side):
                total = None
                for t in range(ways):
                    take = jnp.logical_and(cols[b, t, section] == block, mask[b, t, section] != 0)
                    term = tile_of[t] * jnp.where(take, 1.0, 0.0)
                    total = term if total is None else total + term
                dense[index, pl.ds(pl.multiple_of(b * side, side), side),
                      block * side:(block + 1) * side] = total.astype(BF16)

    def product(t, i, j, k, at):
        index = (1 - i) * 4 + j * 2 + k
        return jnp.dot(dense[index, at, :], slots[i][j][k][t], preferred_element_type=F32)

    def add_product(t, i, j, k):
        if k == 1:
            c_copy(t, i, j, everything).wait_recv()
        term = product(t, i, j, k, everything)
        if (i, j, k) == (1, 0, 0):
            acc[t] = term
        else:
            acc[t] = acc[t] + term

    def p_copy(t):
        return remote(part_out.at[t], part_in.at[t], psend.at[t], precv.at[t], peers["x"][0])

    peer_rows = pl.ds(pl.multiple_of((1 - r) * half, half), half)
    own_rows = pl.ds(pl.multiple_of(r * half, half), half)

    def exchange(t):
        part_out[t] = acc[t, peer_rows, :].astype(BF16)
        p_copy(t).start()
        mixed[t] = acc[t, own_rows, :].astype(BF16)

    def meet(t):
        p_copy(t).wait_recv()
        low = (mixed[t].astype(F32) + part_in[t].astype(F32)).astype(BF16)
        mixed[t] = low
        return jnp.dot(low, weight_v[t * tw:(t + 1) * tw, :], preferred_element_type=F32)

    jobs = [(i, j, k) for i in (1, 0) for j in range(2) for k in range(2)]
    order = [(t, i, ch) for t in range(THIRDS) for i in (1, 0) for ch in range(CHUNKS)]
    lag = 4
    for position, (t, i, ch) in enumerate(order):
        if i == 1 and ch == 0:
            own_step(t)
        if position == 0:
            cols_load.wait()
            mask_load.wait()
            tiles_load.wait()
        z_step(t, i, ch)
        if position >= lag:
            y_step(*order[position - lag])
        step = position % (2 * CHUNKS)
        if t == 0:
            assemble(step)
        elif t < THIRDS - 1:
            add_product(t - 1, *jobs[step])
            if step == 7:
                exchange(t - 1)
        elif step < 4:
            add_product(t - 1, *jobs[2 * step])
            add_product(t - 1, *jobs[2 * step + 1])
            if step == 3:
                exchange(t - 1)
        else:
            if step == 5:
                weight_load.wait()
                bias_load.wait()
                pre_acc[...] = meet(0) + bias_ref[...].reshape(1, width)
            if step > 5:
                add_product(t, *jobs[step - 6])
    last_third = THIRDS - 1
    for behind in range(lag, 0, -1):
        y_step(*order[-behind])
        if behind in (4, 3):
            add_product(last_third, *jobs[6 - behind])
    for t in range(1, last_third):
        pre_acc[...] = pre_acc[...] + meet(t)
    c_copy(last_third, 0, 0, everything).wait_recv()
    c_copy(last_third, 0, 1, everything).wait_recv()

    def finish(at, target):
        total = acc[last_third, at, :]
        for j in range(2):
            for k in range(2):
                total = total + product(last_third, 0, j, k, at)
        target[last_third] = total.astype(BF16)

    finish(peer_rows, part_out)
    p_copy(last_third).start()
    finish(own_rows, mixed)
    for t in range(last_third):
        mixed_t[t] = mixed[t].T
    cot_load.wait()
    pre = pre_acc[...] + meet(last_third)
    mixed_t[last_third] = mixed[last_third].T
    sig = 1.0 / (1.0 + jnp.exp(-pre))
    out_ref[...] = (pre * sig).astype(BF16)
    grad = cot_v[...].astype(F32) * sig * (1.0 + pre * (1.0 - sig))
    glow[...] = grad.astype(BF16)
    bias_rows = jnp.sum(grad.reshape(half // 8, 8, width), axis=0)

    cw = width // 2
    group_rows = tw
    own_cols = pl.ds(pl.multiple_of(c * cw, 128), cw)
    other_cols = pl.ds(pl.multiple_of((1 - c) * cw, 128), cw)

    def grad_part(g, start):
        lanes = pl.ds(pl.multiple_of(start, 128), cw)
        return jnp.dot(mixed_t[g], glow[:, lanes], preferred_element_type=F32)

    def b_send(stage, axis_peers, first):
        copies = []
        for d, device in enumerate(axis_peers):
            copies.append(remote(bstate.at[stage], brecv.at[first + d], bs.at[first + d],
                                 br.at[first + d], device))
            copies[-1].start()
        return copies

    def b_sum(stage, copies, first):
        for copy in copies:
            copy.wait_recv()
        total = bstate[stage] + brecv[first]
        if len(copies) == 3:
            total = total + (brecv[first + 1] + brecv[first + 2])
        bstate[stage + 1] = total

    sent = []
    bstate[0] = bias_rows
    core_copies = []
    for g in range(3):
        at = pl.ds(g * group_rows, group_rows)
        gcore_out[at, :] = grad_part(g, (1 - c) * cw).astype(BF16)
        core_copies.append(remote(gcore_out.at[at], gcore_in.at[at], gcs.at[g], gcr.at[g], other_core))
        core_copies[-1].start()
    b_copies = b_send(0, [other_core], 0)
    sent += core_copies + b_copies
    for g in range(3):
        gacc[pl.ds(g * group_rows, group_rows), :] = grad_part(g, c * cw)

    starts = [g * group_rows for g in range(3)]
    history = [[], [], []]
    flying = [None, None, None]

    def scatter(g, stage):
        axis = ORDERS[g][stage]
        size = part_rows(group_rows, ORDERS[g], stage)
        copies = []
        for d, (device, place) in enumerate(zip(peers[axis], places[axis])):
            at = pl.ds(pl.multiple_of(starts[g] + place * size, size), size)
            gsend[at, :] = gacc[at, :].astype(BF16)
            copies.append(remote(gsend.at[at], rbufs[g][stage].at[d],
                                 rs_s.at[g, stage, d], rs_r.at[g, stage, d], device))
            copies[-1].start()
        flying[g] = copies
        sent.extend(copies)

    def gather(g, stage):
        axis = ORDERS[g][stage]
        size = part_rows(group_rows, ORDERS[g], stage)
        at = pl.ds(pl.multiple_of(starts[g], size), size)
        arriving = []
        for d, (device, place) in enumerate(zip(peers[axis], places[axis])):
            copy = remote(gw_ref.at[at, own_cols], gw_ref.at[at, own_cols], ag_s.at[g, stage, d], ag_r.at[g, stage, d], device)
            copy.start()
            sent.append(copy)
            there = pl.ds(pl.multiple_of(history[g][stage] + place * size, size), size)
            arriving.append((there, remote(gw_ref.at[there, own_cols], gw_ref.at[there, own_cols], ag_s.at[g, stage, d],
                                           ag_r.at[g, stage, d], device)))
        starts[g] = history[g][stage]
        flying[g] = arriving

    def to_core(at):
        remote(gw_ref.at[at, own_cols], gw_ref.at[at, own_cols], fs, fr, other_core).start()

    for g in range(3):
        at = pl.ds(g * group_rows, group_rows)
        core_copies[g].wait_recv()
        gacc[at, :] = gacc[at, :] + gcore_in[at, :].astype(F32)
        scatter(g, 0)
    b_sum(0, b_copies, 0)
    b_first = (1, 2, 3)
    for stage in range(3):
        b_copies = b_send(stage + 1, peers[ORDERS[0][stage]], b_first[stage])
        sent += b_copies
        for g, order_g in enumerate(ORDERS):
            size = part_rows(group_rows, order_g, stage)
            for copy in flying[g]:
                copy.wait_recv()
            keep = starts[g] + mine[order_g[stage]] * size
            at = pl.ds(pl.multiple_of(keep, size), size)
            total = gacc[at, :]
            for d in range(len(flying[g])):
                total = total + rbufs[g][stage][d].astype(F32)
            history[g].append(starts[g])
            starts[g] = keep
            if stage < 2:
                gacc[at, :] = total
                scatter(g, stage + 1)
            else:
                gw_ref[at, own_cols] = total.astype(BF16)
                gather(g, 2)
                to_core(at)
        b_sum(stage + 1, b_copies, b_first[stage])
    for stage in (2, 1, 0):
        for g in range(3):
            arriving = flying[g]
            for _, copy in arriving:
                copy.wait_recv()
            if stage > 0:
                gather(g, stage - 1)
            for there, _ in arriving:
                to_core(there)
    gb_ref[...] = jnp.sum(bstate[4], axis=0)
    remote(gw_ref.at[:, other_cols], gw_ref.at[:, other_cols], fs, fr, other_core).wait_recv()
    remote(gw_ref.at[:, own_cols], gw_ref.at[:, own_cols], fs, fr, other_core).wait_send()

    for t in range(THIRDS):
        for i in range(2):
            waited = w != i if t < THIRDS - 1 else w >= 0

            @pl.when(jnp.logical_and(ups[i], waited))
            def _():
                up_sent(t, i)
            y_copy(t, i, everything, yrecv.at[t, i, 0]).wait_send()
            for j in range(2):
                c_copy(t, i, j, everything).wait_send()

        @pl.when(w == 1)
        def _():
            z_copy(t, 1, everything, zdown.at[t], zrecv.at[t, 1, 0], down).wait_send()
        p_copy(t).wait_send()
    for copy in sent:
        copy.wait_send()


def in_kernel(features, tiles, tile_cols, tile_mask, weight, bias, cotangent):
    rows, width = features.shape
    half = rows // 2
    cw = width // 2
    tw = width // THIRDS
    vmem = pl.BlockSpec(memory_space=pltpu.VMEM)
    hbm = pl.BlockSpec(memory_space=pltpu.HBM)
    dma = pltpu.SemaphoreType.DMA
    rbufs = [
        pltpu.VMEM((WAYS[order[stage]] - 1, part_rows(tw, order, stage), cw), BF16)
        for order in ORDERS
        for stage in range(3)
    ]
    out, grad_weight, grad_bias = pl.pallas_call(
        kernel,
        out_shape=(
            jax.ShapeDtypeStruct((half, width), BF16),
            jax.ShapeDtypeStruct((width, width), BF16),
            jax.ShapeDtypeStruct((width,), F32),
        ),
        in_specs=[hbm] * 7,
        out_specs=(vmem, vmem, vmem),
        scratch_shapes=[pltpu.VMEM((THIRDS, rows, tw), BF16)] * 8
        + [
            pltpu.VMEM(tiles.shape, BF16),
            pltpu.VMEM(weight.shape, BF16),
            pltpu.VMEM(cotangent.shape, BF16),
            pltpu.SMEM((tiles.shape[0], tiles.shape[2], tiles.shape[1]), jnp.int32),
            pltpu.SMEM((tiles.shape[0], tiles.shape[2], tiles.shape[1]), jnp.int32),
            pltpu.VMEM((width,), F32),
            pltpu.VMEM((8, rows, rows), BF16),
            pltpu.VMEM((THIRDS, rows, tw), F32),
            pltpu.VMEM((THIRDS, half, tw), BF16),
            pltpu.VMEM((THIRDS, half, tw), BF16),
            pltpu.VMEM((THIRDS, half, tw), BF16),
            pltpu.VMEM((THIRDS, tw, half), BF16),
            pltpu.VMEM((half, width), F32),
            pltpu.VMEM((half, width), BF16),
            pltpu.VMEM((width, cw), F32),
        ]
        + [pltpu.VMEM((width, cw), BF16)] * 3
        + rbufs
        + [
            pltpu.VMEM((5, 8, width), F32),
            pltpu.VMEM((6, 8, width), F32),
            dma((6 + THIRDS,)), dma((THIRDS, 2, CHUNKS)), dma((THIRDS, 2, CHUNKS)), dma((THIRDS, 4)),
            dma((THIRDS, 2)), dma((THIRDS,)), dma((THIRDS, 2)), dma((THIRDS, 4)),
            dma((THIRDS,)), dma((THIRDS,)), dma((3,)), dma((3,)),
            dma((3, 3, 3)), dma((3, 3, 3)), dma((3, 3, 3)), dma((3, 3, 3)),
            dma, dma, dma((6,)), dma((6,)),
        ],
        compiler_params=pltpu.CompilerParams(
            collective_id=0, has_side_effects=True, vmem_limit_bytes=63 * 1024 * 1024
        ),
    )(features, tiles, tile_cols.transpose(0, 2, 1), tile_mask.transpose(0, 2, 1), weight, bias, cotangent)
    return out, grad_weight.astype(F32), grad_bias


def solution(mesh):
    placed = (
        P("dom", None),
        P("dom", "rep", None, None, None),
        P("dom", "rep", None),
        P("dom", "rep", None),
        P(),
        P(),
        P(("dom", "rep"), None),
    )
    body = in_kernel if (mesh.shape["dom"], mesh.shape["rep"]) == (16, 2) else on_device
    return jax.shard_map(
        body,
        mesh=mesh,
        in_specs=placed,
        out_specs=(P(("dom", "rep"), None), P(), P()),
        check_vma=False,
    )
```
